256 devices in a mesh: dp: 16 (over z, x_hi), expert: 16 (over y, x_lo, core).
Axes of the slice: x: 4 (x_hi: 2, x_lo: 2; x = x_hi * 2 + x_lo), y: 4, z: 8, core: 2. Of those that a mesh axis runs over, the one named last changes fastest.
Arguments:
- latent: bfloat16 [3, 8192, 1536], P(None, 'dp'), may hold values from -6 to 6
- query_grad: bfloat16 [3, 8192, 12288], P(None, 'dp', 'expert'), may hold values from -0.15625 to 0.15625
- momentum: float32 [3, 64, 192, 1536], P(None, 'expert', 'dp'), may hold values from -6 to 6
- weight: float32 [3, 64, 192, 1536], P(None, 'expert', 'dp'), may hold values from -6 to 6
- max_logit: float32 [3, 64], P(None, 'expert'), may hold values from 40 to 400
- owner_list: int32 [3, 64], P(None, 'expert'), may hold values from 0 to 15, as said below
Outputs:
- update: float32 [3, 64, 192, 1536], P(None, 'expert', 'dp')
- new_weight: float32 [3, 64, 192, 1536], P(None, 'expert', 'dp')
- new_momentum: float32 [3, 64, 192, 1536], P(None, 'expert', 'dp')
- owned_updates: bfloat16 [16, 32, 192, 1536], P('expert', 'dp')
The draws below stay inside these ranges and needn't reach their ends.
Inputs may be any that keep to these rules, and one draw needn't show every extreme that they name: `owner_list`: among the 12 matrices of one index of expert no owner is named more than 2 times, and some owner is named exactly 2 times.
All inputs are finite; a program needn't handle non-finite values.
Results may differ from the reference program's by a relative error of at most 0.03.
Values may be sent and summed in bfloat16 or wider, within the bound.
A program may use at most 128 MiB of HBM per device.

```python
import math
import jax
import jax.numpy as jnp
from jax import lax

NOPE = 128
QHEAD = 192
QLORA = 1536
HEADS_DEV = 4
HEADS = 64
LAYERS = 3
TOK_DEV = 512
TOKENS = 8192
CAP = 2
ITERS = 5
N_DP = 16
N_EXPERT = 16


def draw_owner_list(key, part):
    key = jax.random.fold_in(key, 11)
    columns = HEADS // HEADS_DEV
    mats = LAYERS * HEADS_DEV
    paired = max(1, mats - N_DP)
    column_keys = jax.random.split(key, columns)

    def one_column(column_key):
        first_key, second_key = jax.random.split(column_key)
        chosen = jax.random.permutation(first_key, N_DP)
        index = jnp.arange(mats)
        picks = jnp.where(index < 2 * paired, index // 2, index - paired)
        base = chosen[picks]
        order = jax.random.permutation(second_key, mats)
        return base[order]
    table = jax.vmap(one_column)(column_keys)
    table = table.reshape(columns, LAYERS, HEADS_DEV).transpose(1, 0, 2)
    return table.reshape(LAYERS, HEADS).astype(jnp.int32)


def levels(key, shape, cuts, low, high):
    loudness, own = 1.0, jax.random.fold_in(key, 6)
    for axis_at, shards_of in cuts:
        steps = jnp.exp(jax.random.uniform(jax.random.fold_in(own, axis_at), (shards_of,), jnp.float32, low / len(cuts), high / len(cuts)))
        loudness = loudness * jnp.repeat(steps, shape[axis_at] // shards_of).reshape([-1 if axis == axis_at else 1 for axis in range(len(shape))])
    return loudness


def scatter_about(own_key, shape, width, most, pieces=(), kind=jnp.bfloat16):
    gain = levels(own_key, shape, pieces, -0.22, 0.18) if pieces else 1.0
    values = jax.random.normal(own_key, shape, jnp.float32) * width * gain
    return jnp.minimum(jnp.maximum(values, -most), most).astype(kind)


def setup_inputs(seed: int = 0) -> dict:
    key_of = jax.random.split(jax.random.key(seed), 7)
    latent = scatter_about(key_of[0], (LAYERS, TOKENS, QLORA), 1.0, 6.0, ((1, 16),))
    query_grad = scatter_about(key_of[1], (LAYERS, TOKENS, HEADS * QHEAD), (TOKENS ** -0.5), 0.15625, ((1, 16), (2, 16)))
    momentum = scatter_about(key_of[2], (LAYERS, HEADS, QHEAD, QLORA), 1.0, 6.0, ((1, 16), (2, 16)), jnp.float32)
    weight = scatter_about(key_of[3], (LAYERS, HEADS, QHEAD, QLORA), 1.0, 6.0, ((1, 16), (2, 16)), jnp.float32)
    max_logit = jnp.clip(jnp.exp(math.log(400.0) - 2.3025851 * jax.random.uniform(key_of[4], (LAYERS, HEADS), jnp.float32) ** levels(key_of[4], (LAYERS, HEADS), ((1, 16),), -0.2, 0.2)), 40.0, 400.0)
    owner_list = draw_owner_list(jax.random.fold_in(key_of[6], 71), 0)
    return {"latent": latent, "query_grad": query_grad, "momentum": momentum, "weight": weight, "max_logit": max_logit, "owner_list": owner_list}


DECAY_RATE = 0.95
EPSILON = 1e-07
COEF_LINEAR = 3.4445
COEF_CUBIC = -4.775
COEF_QUINTIC = 2.0315
LEARN_RATE = 0.02
WEIGHT_DECAY = 0.1
CLIP_LIMIT = 100.0
RMS_FACTOR = 0.2

def ns_step(iterate, gram_matrix):
    gram_square = jnp.einsum('hij,hjk->hik', gram_matrix, gram_matrix, precision=lax.Precision.HIGHEST)
    mixing = COEF_CUBIC * gram_matrix + COEF_QUINTIC * gram_square
    return COEF_LINEAR * iterate + jnp.einsum('hij,hjk->hik', mixing, iterate, precision=lax.Precision.HIGHEST)

def reference(latent, query_grad, momentum, weight, max_logit, owner_list):

    def layer_grad(pair):
        blocks_x = pair[0].reshape(N_DP, TOK_DEV, QLORA)
        blocks_g = pair[1].reshape(N_DP, TOK_DEV, HEADS, QHEAD)

        def add_block(running, blocks):
            partial_value = jnp.einsum('thr,tk->hrk', blocks[1].astype(jnp.float32), blocks[0].astype(jnp.float32))
            partial_value = lax.optimization_barrier(partial_value.astype(jnp.bfloat16)).astype(jnp.float32)
            return (running + partial_value, None)
        running, unused = lax.scan(add_block, jnp.zeros((HEADS, QHEAD, QLORA), jnp.float32), (blocks_x, blocks_g))
        return running
    head_grad = lax.map(layer_grad, (latent, query_grad))
    new_momentum = DECAY_RATE * momentum + head_grad
    values = new_momentum.reshape(LAYERS * HEADS, QHEAD, QLORA).astype(jnp.bfloat16).astype(jnp.float32)
    norms = jnp.sqrt(lax.optimization_barrier(jnp.sum(values * values, axis=(1, 2))))
    iterate = values / (norms + EPSILON)[:, None, None]
    for sweep in range(ITERS):
        gram_matrix = jnp.einsum('hik,hjk->hij', iterate, iterate, precision=lax.Precision.HIGHEST)
        iterate = ns_step(iterate, gram_matrix)
    update = iterate.reshape(LAYERS, HEADS, QHEAD, QLORA)
    clip_factor = jnp.minimum(1.0, CLIP_LIMIT / max_logit)
    row_index = jnp.arange(QHEAD)
    row_scale = jnp.where(row_index[None, None, :] < NOPE, jnp.sqrt(clip_factor)[:, :, None], clip_factor[:, :, None])
    step_scale = LEARN_RATE * RMS_FACTOR * math.sqrt(max(QHEAD, QLORA))
    new_weight = (weight * (1.0 - LEARN_RATE * WEIGHT_DECAY) - step_scale * update) * row_scale[:, :, :, None]
    mats = LAYERS * HEADS_DEV
    owners = owner_list.reshape(LAYERS, N_EXPERT, HEADS_DEV).transpose(1, 0, 2).reshape(N_EXPERT, mats)
    same_owner = owners[:, :, None] == owners[:, None, :]
    earlier = jnp.arange(mats)[None, :] < jnp.arange(mats)[:, None]
    slot_rank = lax.optimization_barrier(jnp.sum((same_owner & earlier[None]).astype(jnp.int32), axis=2))
    placing = (owners[:, None, None, :] == jnp.arange(N_DP)[None, :, None, None]) & (slot_rank[:, None, None, :] == jnp.arange(CAP)[None, None, :, None])
    grouped = update.reshape(LAYERS, N_EXPERT, HEADS_DEV, QHEAD, QLORA).transpose(1, 0, 2, 3, 4).reshape(N_EXPERT, mats, QHEAD, QLORA)
    owned_updates = jnp.einsum('cosj,cjik->cosik', placing.astype(jnp.float32), grouped, precision=lax.Precision.HIGHEST)
    owned_updates = owned_updates.reshape(N_EXPERT, N_DP * CAP, QHEAD, QLORA).astype(jnp.bfloat16)
    return (update, new_weight, new_momentum, owned_updates)
```

```python
import functools
import math

import jax
import jax.numpy as jnp
import numpy as np
from jax import lax
from jax.experimental import pallas as pl
from jax.experimental.pallas import tpu as pltpu
from jax.sharding import PartitionSpec as P

NOPE = 128
CAP = 2
ITERS = 5
X_HI = 2

DECAY_RATE = 0.95
EPSILON = 1e-07
COEF_LINEAR = 3.4445
COEF_CUBIC = -4.775
COEF_QUINTIC = 2.0315
LEARN_RATE = 0.02
WEIGHT_DECAY = 0.1
CLIP_LIMIT = 100.0
RMS_FACTOR = 0.2

MESH = pl.DeviceIdType.MESH
F32 = jnp.float32
BF16 = jnp.bfloat16


def swap_matrix(first, second, inner):
    order = np.arange(first * second * inner).reshape(first, second, inner)
    picked = order.transpose(1, 0, 2).reshape(-1)
    table = np.zeros((picked.size, picked.size), np.float32)
    table[np.arange(picked.size), picked] = 1.0
    return table


def remote(src, dst, send_sem, recv_sem, dp):
    return pltpu.make_async_remote_copy(
        src_ref=src,
        dst_ref=dst,
        send_sem=send_sem,
        recv_sem=recv_sem,
        device_id={"dp": dp},
        device_id_type=MESH,
    )


def full_dot(left, right):
    return jnp.dot(left, right, precision=lax.Precision.HIGHEST, preferred_element_type=F32)


def polynomial(gram):
    size = gram.shape[0]
    rows = lax.broadcasted_iota(jnp.int32, (size, size), 0)
    columns = lax.broadcasted_iota(jnp.int32, (size, size), 1)
    eye = jnp.where(rows == columns, 1.0, 0.0).astype(F32)
    total = None
    for sweep in range(ITERS):
        mixing = COEF_LINEAR * eye + COEF_CUBIC * gram + COEF_QUINTIC * full_dot(gram, gram)
        total = mixing if total is None else full_dot(mixing, total)
        if sweep < ITERS - 1:
            gram = full_dot(full_dot(mixing, gram), mixing)
    return total


def kernel(
    group,
    latent_ref, grad_ref, momentum_ref, swap_ref, unswap_ref, small_ref, pick_ref, spot_ref,
    new_momentum_ref, owned_ref, update_ref,
    cot, part, recv_z, recv_x, total, blocks, outgoing, incoming, shuffled, back, returned,
    send_z, got_z, send_x, got_x, send_a, got_a, send_b, got_b,
):
    layers, heads, rows_q, width = momentum_ref.shape
    rows = heads * rows_q
    mats = layers * heads
    ring = group // X_HI
    quarter = width // 4
    full_rows = rows_q * group
    me = lax.axis_index("dp")
    z = me // X_HI
    side = me % X_HI
    up = lax.rem(z + 1, ring) * X_HI + side
    down = lax.rem(z + ring - 1, ring) * X_HI + side
    partner = z * X_HI + 1 - side

    barrier = pltpu.get_barrier_semaphore()
    for step in range(1, group):
        pl.semaphore_signal(
            barrier, inc=1, device_id={"dp": lax.rem(me + step, group)}, device_id_type=MESH
        )
    pl.semaphore_wait(barrier, group - 1)

    def ring_copy(layer, way, step):
        if way == 0:
            chunk = lax.rem(z - 1 - step + 2 * ring, ring)
        else:
            chunk = lax.rem(z + 1 + step, ring)
        return remote(
            part.at[layer, chunk * X_HI + way],
            recv_z.at[step, layer, way],
            send_z.at[step, layer, way],
            got_z.at[step, layer, way],
            up if way == 0 else down,
        )

    for layer in range(layers):
        cot[...] = lax.dot_general(
            swap_ref[...], grad_ref[layer], (((1,), (1,)), ((), ())), preferred_element_type=F32
        ).astype(BF16)

        @pl.loop(0, width // 256)
        def _(tile):
            columns = pl.ds(pl.multiple_of(tile * 256, 256), 256)
            product = jnp.dot(cot[...], latent_ref[layer, :, columns], preferred_element_type=F32)
            part[layer, :, :, columns] = product.astype(BF16).reshape(group, rows, 256)

        for way in range(2):
            ring_copy(layer, way, 0).start()

    def pair_copy(layer):
        return remote(
            part.at[layer, partner], recv_x.at[layer], send_x.at[layer], got_x.at[layer], partner
        )

    for step in range(ring - 1):
        for layer in range(layers):
            for way in range(2):
                ring_copy(layer, way, step).wait_recv()
                if step < ring - 2:
                    if way == 0:
                        chunk = lax.rem(z - 2 - step + 2 * ring, ring)
                    else:
                        chunk = lax.rem(z + 2 + step, ring)
                    spot = chunk * X_HI + way
                    part[layer, spot] = (
                        part[layer, spot].astype(F32) + recv_z[step, layer, way].astype(F32)
                    ).astype(BF16)
                    ring_copy(layer, way, step + 1).start()
            if step == ring - 2:
                part[layer, partner] = (
                    part[layer, partner].astype(F32) + recv_z[step, layer, 1 - side].astype(F32)
                ).astype(BF16)
                pair_copy(layer).start()

    for layer in range(layers):
        pair_copy(layer).wait_recv()
        total[...] = (
            part[layer, me].astype(F32)
            + recv_z[ring - 2, layer, side].astype(F32)
            + recv_x[layer].astype(F32)
        )
        for head in range(heads):
            span = pl.ds(head * rows_q, rows_q)
            fresh = DECAY_RATE * momentum_ref[layer, head] + total[span, :]
            new_momentum_ref[layer, head] = fresh
            total[span, :] = fresh
        stacked = jnp.concatenate(
            [total[:, q * quarter : (q + 1) * quarter].astype(BF16) for q in range(4)], axis=0
        )
        turned = jnp.dot(small_ref[...], stacked, preferred_element_type=F32).astype(BF16)
        blocks[layer * heads : (layer + 1) * heads] = turned.reshape(heads, rows, quarter)
    blocks[mats] = jnp.zeros((rows, quarter), BF16)

    def out_copy(slot, step):
        peer = lax.rem(me + step, group)
        return remote(
            outgoing.at[slot, peer],
            incoming.at[slot, me],
            send_a.at[slot, step],
            got_a.at[slot, step],
            peer,
        )

    def back_copy(slot, step):
        peer = lax.rem(me + step, group)
        return remote(
            back.at[slot, peer],
            returned.at[slot, me],
            send_b.at[slot, step],
            got_b.at[slot, step],
            peer,
        )

    for slot in range(CAP):
        incoming[slot, me] = blocks[pick_ref[slot, me]]

        @pl.loop(1, group)
        def _(step):
            peer = lax.rem(me + step, group)
            outgoing[slot, peer] = blocks[pick_ref[slot, peer]]
            out_copy(slot, step).start()

    for slot in range(CAP):

        @pl.loop(1, group)
        def _(step):
            out_copy(slot, step).wait_recv()

        shuffled[...] = jnp.dot(
            unswap_ref[...],
            incoming[slot].reshape(group * rows, quarter),
            preferred_element_type=F32,
        ).astype(BF16)
        gram = jnp.zeros((full_rows, full_rows), F32)
        for q in range(4):
            piece = shuffled[q * full_rows : (q + 1) * full_rows]
            gram = gram + lax.dot_general(
                piece, piece, (((1,), (1,)), ((), ())), preferred_element_type=F32
            )
        on_diagonal = lax.broadcasted_iota(jnp.int32, gram.shape, 0) == lax.broadcasted_iota(
            jnp.int32, gram.shape, 1
        )
        squares = jnp.sum(
            jnp.sum(jnp.where(on_diagonal, gram, 0.0), axis=1, keepdims=True), axis=0, keepdims=True
        )
        scale = 1.0 / (jnp.sqrt(squares) + EPSILON)
        mixed = polynomial(gram * scale * scale) * scale
        high = mixed.astype(BF16)
        low = (mixed - high.astype(F32)).astype(BF16)
        for q in range(4):
            span = slice(q * full_rows, (q + 1) * full_rows)
            piece = shuffled[span]
            result = (
                jnp.dot(high, piece, preferred_element_type=F32)
                + jnp.dot(low, piece, preferred_element_type=F32)
            ).astype(BF16)
            owned_ref[slot, :, q * quarter : (q + 1) * quarter] = result
            shuffled[span] = result
        back[slot] = (
            jnp.dot(swap_ref[...], shuffled[...], preferred_element_type=F32)
            .astype(BF16)
            .reshape(group, rows, quarter)
        )
        returned[slot, me] = back[slot, me]

        @pl.loop(1, group)
        def _(step):
            back_copy(slot, step).start()

    for slot in range(CAP):

        @pl.loop(1, group)
        def _(step):
            back_copy(slot, step).wait_recv()

    for layer in range(layers):
        gathered = jnp.concatenate(
            [
                returned[spot_ref[0, layer * heads + head], spot_ref[1, layer * heads + head]]
                for head in range(heads)
            ],
            axis=0,
        )
        turned = jnp.dot(small_ref[...], gathered, preferred_element_type=F32)
        for q in range(4):
            update_ref[layer, :, q * quarter : (q + 1) * quarter] = turned[
                q * rows : (q + 1) * rows
            ]

    for layer in range(layers):
        for step in range(ring - 1):
            for way in range(2):
                ring_copy(layer, way, step).wait_send()
        pair_copy(layer).wait_send()
    for slot in range(CAP):

        @pl.loop(1, group)
        def _(step):
            out_copy(slot, step).wait_send()
            back_copy(slot, step).wait_send()


def on_device(latent, query_grad, momentum, weight, max_logit, owner_list):
    group = lax.axis_size("dp")
    layers, heads, rows_q, width = momentum.shape
    mats = layers * heads
    full_rows = rows_q * group
    rows = heads * rows_q
    quarter = width // 4
    ring = group // X_HI
    owners = owner_list.reshape(mats)
    same_owner = owners[:, None] == owners[None, :]
    earlier = jnp.arange(mats)[None, :] < jnp.arange(mats)[:, None]
    slot_rank = jnp.sum((same_owner & earlier).astype(jnp.int32), axis=1)
    placing = (owners[None, None, :] == jnp.arange(group)[None, :, None]) & (
        slot_rank[None, None, :] == jnp.arange(CAP)[:, None, None]
    )
    pick = mats + jnp.sum(jnp.where(placing, jnp.arange(mats) - mats, 0), axis=2).astype(jnp.int32)
    spot = jnp.stack([slot_rank, owners]).astype(jnp.int32)

    swap = jnp.asarray(swap_matrix(heads, group, rows_q), BF16)
    unswap = jnp.asarray(swap_matrix(group, heads, rows_q), BF16)
    small = jnp.asarray(swap_matrix(heads, 4, rows_q), BF16)

    vmem = pl.BlockSpec(memory_space=pltpu.VMEM)
    smem = pl.BlockSpec(memory_space=pltpu.SMEM)
    new_momentum, owned, update = pl.pallas_call(
        functools.partial(kernel, group),
        out_shape=(
            jax.ShapeDtypeStruct(momentum.shape, F32),
            jax.ShapeDtypeStruct((CAP, full_rows, width), BF16),
            jax.ShapeDtypeStruct((layers, rows, width), F32),
        ),
        in_specs=[vmem] * 6 + [smem] * 2,
        out_specs=(vmem, vmem, vmem),
        scratch_shapes=[
            pltpu.VMEM((heads * full_rows, latent.shape[1]), BF16),
            pltpu.VMEM((layers, group, rows, width), BF16),
            pltpu.VMEM((ring - 1, layers, 2, rows, width), BF16),
            pltpu.VMEM((layers, rows, width), BF16),
            pltpu.VMEM((rows, width), F32),
            pltpu.VMEM((mats + 1, rows, quarter), BF16),
            pltpu.VMEM((CAP, group, rows, quarter), BF16),
            pltpu.VMEM((CAP, group, rows, quarter), BF16),
            pltpu.VMEM((group * rows, quarter), BF16),
            pltpu.VMEM((CAP, group, rows, quarter), BF16),
            pltpu.VMEM((CAP, group, rows, quarter), BF16),
            pltpu.SemaphoreType.DMA((ring - 1, layers, 2)),
            pltpu.SemaphoreType.DMA((ring - 1, layers, 2)),
            pltpu.SemaphoreType.DMA((layers,)),
            pltpu.SemaphoreType.DMA((layers,)),
            pltpu.SemaphoreType.DMA((CAP, group)),
            pltpu.SemaphoreType.DMA((CAP, group)),
            pltpu.SemaphoreType.DMA((CAP, group)),
            pltpu.SemaphoreType.DMA((CAP, group)),
        ],
        compiler_params=pltpu.CompilerParams(
            collective_id=0, has_side_effects=True, vmem_limit_bytes=56 * 2**20
        ),
    )(latent, query_grad, momentum, swap, unswap, small, pick, spot)

    update = update.reshape(momentum.shape)
    step_scale = LEARN_RATE * RMS_FACTOR * math.sqrt(max(full_rows, width))
    clip_factor = jnp.minimum(1.0, CLIP_LIMIT / max_logit)
    row_index = lax.axis_index("dp") * rows_q + jnp.arange(rows_q)
    row_scale = jnp.where(
        row_index[None, None, :] < NOPE, jnp.sqrt(clip_factor)[:, :, None], clip_factor[:, :, None]
    )
    new_weight = (weight * (1.0 - LEARN_RATE * WEIGHT_DECAY) - step_scale * update) * row_scale[
        :, :, :, None
    ]
    return update, new_weight, new_momentum, owned[None]


def solution(mesh):
    placed = (
        P(None, "dp", None),
        P(None, "dp", "expert"),
        P(None, "expert", "dp", None),
        P(None, "expert", "dp", None),
        P(None, "expert"),
        P(None, "expert"),
    )
    return jax.shard_map(
        on_device,
        mesh=mesh,
        in_specs=placed,
        out_specs=(
            P(None, "expert", "dp", None),
            P(None, "expert", "dp", None),
            P(None, "expert", "dp", None),
            P("expert", "dp", None, None),
        ),
        check_vma=False,
    )
```

```python
import functools
import math

import jax
import jax.numpy as jnp
import numpy as np
from jax import lax
from jax.experimental import pallas as pl
from jax.experimental.pallas import tpu as pltpu
from jax.sharding import PartitionSpec as P

NOPE = 128
CAP = 2
ITERS = 5
X_HI = 2

DECAY_RATE = 0.95
EPSILON = 1e-07
COEF_LINEAR = 3.4445
COEF_CUBIC = -4.775
COEF_QUINTIC = 2.0315
LEARN_RATE = 0.02
WEIGHT_DECAY = 0.1
CLIP_LIMIT = 100.0
RMS_FACTOR = 0.2

MESH = pl.DeviceIdType.MESH
F32 = jnp.float32
BF16 = jnp.bfloat16


def reorder_matrix(shape, axes):
    picked = np.arange(math.prod(shape)).reshape(shape).transpose(axes).reshape(-1)
    table = np.zeros((picked.size, picked.size), np.float32)
    table[np.arange(picked.size), picked] = 1.0
    return table


def remote(src, dst, send_sem, recv_sem, dp):
    return pltpu.make_async_remote_copy(
        src_ref=src,
        dst_ref=dst,
        send_sem=send_sem,
        recv_sem=recv_sem,
        device_id={"dp": dp},
        device_id_type=MESH,
    )


def full_dot(left, right):
    return jnp.dot(left, right, precision=lax.Precision.HIGHEST, preferred_element_type=F32)


def polynomial(gram):
    size = gram.shape[0]
    rows = lax.broadcasted_iota(jnp.int32, (size, size), 0)
    columns = lax.broadcasted_iota(jnp.int32, (size, size), 1)
    eye = jnp.where(rows == columns, 1.0, 0.0).astype(F32)
    total = None
    for sweep in range(ITERS):
        mixing = COEF_LINEAR * eye + COEF_CUBIC * gram + COEF_QUINTIC * full_dot(gram, gram)
        total = mixing if total is None else full_dot(mixing, total)
        if sweep < ITERS - 1:
            gram = full_dot(full_dot(mixing, gram), mixing)
    return total


def kernel(
    group,
    latent_hbm, grad_hbm, momentum_hbm, by_row_hbm, gather_hbm, spread_hbm, split_hbm, join_hbm, owner_ref,
    new_momentum_ref, owned_ref, update_ref,
    latent_ref, grad_ref, momentum_ref, by_row_ref, gather_ref, spread_ref, split_ref, join_ref,
    cot, part_a, part_b, part_x, ring_a, ring_b, ring_x, cross_x, pair_a, pair_b,
    total, turned, pick, blocks, outgoing, incoming, shuffled, back, returned,
    load_sem, send_a, got_a, send_b, got_b, send_x, got_x, send_c, got_c, send_p, got_p,
    send_out, got_out, send_back, got_back,
):
    layers, rows_q, heads, width = momentum_ref.shape
    rows = heads * rows_q
    mats = layers * heads
    ring = group // X_HI
    quarter = width // 4
    half = width // 2
    narrow = part_b.shape[-1]
    extra = part_x.shape[-1] - half
    full_rows = rows_q * group
    me = lax.axis_index("dp")
    z = me // X_HI
    side = me % X_HI
    up = lax.rem(z + 1, ring) * X_HI + side
    down = lax.rem(z + ring - 1, ring) * X_HI + side
    partner = z * X_HI + 1 - side

    barrier = pltpu.get_barrier_semaphore()
    for peer in (up, down, partner):
        pl.semaphore_signal(barrier, inc=1, device_id={"dp": peer}, device_id_type=MESH)

    loads = {}
    for number, (name, src, dst) in enumerate(
        [
            ("by_row", by_row_hbm, by_row_ref),
            ("grad0", grad_hbm.at[0], grad_ref.at[0]),
            ("latent0", latent_hbm.at[0], latent_ref.at[0]),
            ("grad2", grad_hbm.at[2], grad_ref.at[2]),
            ("latent2", latent_hbm.at[2], latent_ref.at[2]),
            ("grad1", grad_hbm.at[1], grad_ref.at[1]),
            ("latent1", latent_hbm.at[1], latent_ref.at[1]),
            ("momentum", momentum_hbm, momentum_ref),
            ("split", split_hbm, split_ref),
            ("gather", gather_hbm, gather_ref),
            ("spread", spread_hbm, spread_ref),
            ("join", join_hbm, join_ref),
        ]
    ):
        loads[name] = pltpu.make_async_copy(src, dst, load_sem.at[number])
        loads[name].start()

    def products(layer, keep):
        loads["grad%d" % layer].wait()
        cot[...] = lax.dot_general(
            by_row_ref[...], grad_ref[layer], (((1,), (1,)), ((), ())), preferred_element_type=F32
        ).astype(BF16)
        loads["latent%d" % layer].wait()
        for first in range(0, group, 4):
            product = jnp.dot(
                cot[first * rows : (first + 4) * rows], latent_ref[layer], preferred_element_type=F32
            )
            keep(slice(first, first + 4), product.astype(BF16).reshape(4, rows, width))

    def keep_0(blocks_of, product):
        part_a[blocks_of] = product

    def keep_1(blocks_of, product):
        part_b[blocks_of] = product[:, :, :narrow]
        for way in range(2):
            begin = narrow + way * extra
            part_x[way, blocks_of, :, half:] = product[:, :, begin : begin + extra]

    def keep_2(blocks_of, product):
        for way in range(2):
            part_x[way, blocks_of, :, :half] = product[:, :, way * half : (way + 1) * half]

    def chunk_at(way, step):
        if way == 0:
            return lax.rem(z - 1 - step + 2 * ring, ring)
        return lax.rem(z + 1 + step, ring)

    def ring_copy(kind, way, step):
        chunk = chunk_at(way, step)
        src, dst, send, got = {
            "a": (part_a.at[chunk * X_HI + way], ring_a, send_a, got_a),
            "b": (part_b.at[chunk * X_HI + way], ring_b, send_b, got_b),
            "x": (part_x.at[way, chunk * X_HI + side], ring_x, send_x, got_x),
        }[kind]
        return remote(
            src, dst.at[step, way], send.at[step, way], got.at[step, way], up if way == 0 else down
        )

    def cross_copy(way, step):
        chunk = chunk_at(way, step)
        return remote(
            part_x.at[way, chunk * X_HI + 1 - side],
            cross_x.at[way, chunk],
            send_c.at[step, way],
            got_c.at[step, way],
            partner,
        )

    def pair_copy(kind):
        number, src, dst = {"a": (0, part_a, pair_a), "b": (1, part_b, pair_b)}[kind]
        return remote(src.at[partner], dst, send_p.at[number], got_p.at[number], partner)

    def ring_step(kind, way, step):
        if step >= 0:
            ring_copy(kind, way, step).wait_recv()
        if kind == "x":
            cross_copy(way, step + 1).wait_recv()
        if step == ring - 2:
            return
        chunk = chunk_at(way, step + 1)
        if kind == "x":
            spot = chunk * X_HI + side
            value = part_x[way, spot].astype(F32) + cross_x[way, chunk].astype(F32)
            if step >= 0:
                value = value + ring_x[step, way].astype(F32)
            part_x[way, spot] = value.astype(BF16)
        elif step >= 0:
            mine, came = {"a": (part_a, ring_a), "b": (part_b, ring_b)}[kind]
            spot = chunk * X_HI + way
            mine[spot] = (mine[spot].astype(F32) + came[step, way].astype(F32)).astype(BF16)
        ring_copy(kind, way, step + 1).start()

    def pair_step(kind):
        mine, came = {"a": (part_a, ring_a), "b": (part_b, ring_b)}[kind]
        mine[partner] = (
            mine[partner].astype(F32) + came[ring - 2, 1 - side].astype(F32)
        ).astype(BF16)
        pair_copy(kind).start()

    loads["by_row"].wait()
    products(0, keep_0)
    pl.semaphore_wait(barrier, 3)
    for way in range(2):
        ring_step("a", way, -1)
    products(2, keep_2)
    products(1, keep_1)
    for way in range(2):
        ring_step("b", way, -1)
    for step in range(3):
        for way in range(2):
            cross_copy(way, step).start()

    owner_of = [owner_ref[m // heads, m % heads] for m in range(mats)]
    slot_of = []
    for m in range(mats):
        slot = jnp.int32(0)
        for earlier in range(m):
            slot = slot + jnp.where(owner_of[earlier] == owner_of[m], 1, 0)
        slot_of.append(slot)

    @pl.loop(0, group)
    def _(owner):
        for slot in range(CAP):
            found = jnp.int32(mats)
            for m in range(mats):
                found = jnp.where((owner_of[m] == owner) & (slot_of[m] == slot), m, found)
            pick[slot, owner] = found

    for way in range(2):
        ring_step("a", way, 0)
    for way in range(2):
        ring_step("x", way, -1)
    for way in range(2):
        ring_step("b", way, 0)
    for step in range(1, ring - 1):
        if step + 2 < ring:
            for way in range(2):
                cross_copy(way, step + 2).start()
        for way in range(2):
            ring_step("a", way, step)
        if step == ring - 2:
            pair_step("a")
        for way in range(2):
            ring_step("x", way, step - 1)
        for way in range(2):
            ring_step("b", way, step)
        if step == ring - 2:
            pair_step("b")
    for way in range(2):
        ring_step("x", way, ring - 2)

    loads["momentum"].wait()
    loads["split"].wait()

    def last_sum(kind):
        mine, came, other = {"a": (part_a, ring_a, pair_a), "b": (part_b, ring_b, pair_b)}[kind]
        pair_copy(kind).wait_recv()
        return mine[me].astype(F32) + came[ring - 2, side].astype(F32) + other[...].astype(F32)

    def last_sum_x(way, columns):
        return (
            part_x[way, me, :, columns].astype(F32)
            + cross_x[way, z, :, columns].astype(F32)
            + ring_x[ring - 2, way, :, columns].astype(F32)
        )

    for layer in (2, 0, 1):
        if layer == 2:
            for way in range(2):
                total[:, way * half : (way + 1) * half] = last_sum_x(way, slice(0, half))
        elif layer == 0:
            total[...] = last_sum("a")
        else:
            total[:, :narrow] = last_sum("b")
            for way in range(2):
                begin = narrow + way * extra
                total[:, begin : begin + extra] = last_sum_x(way, slice(half, half + extra))
        for row in range(rows_q):
            span = slice(row * heads, (row + 1) * heads)
            fresh = DECAY_RATE * momentum_ref[layer, row] + total[span, :]
            new_momentum_ref[layer, row] = fresh
            total[span, :] = fresh
        stacked = jnp.concatenate(
            [total[:, q * quarter : (q + 1) * quarter].astype(BF16) for q in range(4)], axis=0
        )
        blocks[layer * heads : (layer + 1) * heads] = (
            jnp.dot(split_ref[...], stacked, preferred_element_type=F32)
            .astype(BF16)
            .reshape(heads, rows, quarter)
        )
    blocks[mats] = jnp.zeros((rows, quarter), BF16)

    def out_copy(slot, step):
        peer = lax.rem(me + step, group)
        return remote(
            outgoing.at[slot, peer],
            incoming.at[slot, me],
            send_out.at[slot, step],
            got_out.at[slot, step],
            peer,
        )

    def back_copy(slot, step):
        peer = lax.rem(me + step, group)
        return remote(
            back.at[slot, peer],
            returned.at[slot, me],
            send_back.at[slot, step],
            got_back.at[slot, step],
            peer,
        )

    for slot in range(CAP):

        @pl.loop(1, group)
        def _(step):
            peer = lax.rem(me + step, group)
            outgoing[slot, peer] = blocks[pick[slot, peer]]
            out_copy(slot, step).start()

        incoming[slot, me] = blocks[pick[slot, me]]

    loads["gather"].wait()
    loads["spread"].wait()
    loads["join"].wait()
    for slot in range(CAP):

        @pl.loop(1, group)
        def _(step):
            out_copy(slot, step).wait_recv()

        shuffled[...] = jnp.dot(
            gather_ref[...],
            incoming[slot].reshape(group * rows, quarter),
            preferred_element_type=F32,
        ).astype(BF16)
        gram = jnp.zeros((full_rows, full_rows), F32)
        for q in range(4):
            piece = shuffled[q * full_rows : (q + 1) * full_rows]
            gram = gram + lax.dot_general(
                piece, piece, (((1,), (1,)), ((), ())), preferred_element_type=F32
            )
        on_diagonal = lax.broadcasted_iota(jnp.int32, gram.shape, 0) == lax.broadcasted_iota(
            jnp.int32, gram.shape, 1
        )
        squares = jnp.sum(
            jnp.sum(jnp.where(on_diagonal, gram, 0.0), axis=1, keepdims=True), axis=0, keepdims=True
        )
        scale = 1.0 / (jnp.sqrt(squares) + EPSILON)
        mixed = polynomial(gram * scale * scale) * scale
        high = mixed.astype(BF16)
        low = (mixed - high.astype(F32)).astype(BF16)
        for q in range(4):
            span = slice(q * full_rows, (q + 1) * full_rows)
            piece = shuffled[span]
            result = (
                jnp.dot(high, piece, preferred_element_type=F32)
                + jnp.dot(low, piece, preferred_element_type=F32)
            ).astype(BF16)
            owned_ref[slot, :, q * quarter : (q + 1) * quarter] = result
            shuffled[span] = result
        back[slot] = (
            jnp.dot(spread_ref[...], shuffled[...], preferred_element_type=F32)
            .astype(BF16)
            .reshape(group, rows, quarter)
        )

        @pl.loop(1, group)
        def _(step):
            back_copy(slot, step).start()

        returned[slot, me] = back[slot, me]

    for slot in range(CAP):

        @pl.loop(1, group)
        def _(step):
            back_copy(slot, step).wait_recv()

    for layer in range(layers):
        gathered = jnp.concatenate(
            [
                returned[
                    jnp.minimum(slot_of[layer * heads + head], CAP - 1), owner_of[layer * heads + head]
                ]
                for head in range(heads)
            ],
            axis=0,
        )
        turned[...] = jnp.dot(join_ref[...], gathered, preferred_element_type=F32)
        for row in range(rows_q):
            for q in range(4):
                begin = q * rows + row * heads
                update_ref[layer, row, :, q * quarter : (q + 1) * quarter] = turned[
                    begin : begin + heads, :
                ]

    for way in range(2):
        for step in range(ring - 1):
            for kind in "abx":
                ring_copy(kind, way, step).wait_send()
        for step in range(ring):
            cross_copy(way, step).wait_send()
    for kind in "ab":
        pair_copy(kind).wait_send()
    for slot in range(CAP):

        @pl.loop(1, group)
        def _(step):
            out_copy(slot, step).wait_send()
            back_copy(slot, step).wait_send()


def on_device(latent, query_grad, momentum, weight, max_logit, owner_list):
    group = lax.axis_size("dp")
    layers, heads, rows_q, width = momentum.shape
    mats = layers * heads
    full_rows = rows_q * group
    rows = heads * rows_q
    quarter = width // 4
    half = width // 2
    ring = group // X_HI
    extra = width // 4
    narrow = width - 2 * extra
    wide = half + extra

    by_row = jnp.asarray(reorder_matrix((heads, group, rows_q), (1, 2, 0)), BF16)
    gather = jnp.asarray(reorder_matrix((group, 4, rows_q), (1, 0, 2)), BF16)
    spread = jnp.asarray(reorder_matrix((4, group, rows_q), (1, 0, 2)), BF16)
    split = jnp.asarray(reorder_matrix((4 * rows_q, heads), (1, 0)), BF16)
    join = jnp.asarray(reorder_matrix((heads, 4 * rows_q), (1, 0)), BF16)

    vmem = pl.BlockSpec(memory_space=pltpu.VMEM)
    smem = pl.BlockSpec(memory_space=pltpu.SMEM)
    hbm = pl.BlockSpec(memory_space=pl.ANY)
    by_rows = (layers, rows_q, heads, width)
    dma = pltpu.SemaphoreType.DMA
    new_momentum, owned, update = pl.pallas_call(
        functools.partial(kernel, group),
        out_shape=(
            jax.ShapeDtypeStruct(by_rows, F32),
            jax.ShapeDtypeStruct((CAP, full_rows, width), BF16),
            jax.ShapeDtypeStruct(by_rows, F32),
        ),
        in_specs=[hbm] * 8 + [smem],
        out_specs=(vmem, vmem, vmem),
        scratch_shapes=[
            pltpu.VMEM(latent.shape, BF16),
            pltpu.VMEM(query_grad.shape, BF16),
            pltpu.VMEM(by_rows, F32),
            pltpu.VMEM(by_row.shape, BF16),
            pltpu.VMEM(gather.shape, BF16),
            pltpu.VMEM(spread.shape, BF16),
            pltpu.VMEM(split.shape, BF16),
            pltpu.VMEM(join.shape, BF16),
            pltpu.VMEM((heads * full_rows, latent.shape[1]), BF16),
            pltpu.VMEM((group, rows, width), BF16),
            pltpu.VMEM((group, rows, narrow), BF16),
            pltpu.VMEM((2, group, rows, wide), BF16),
            pltpu.VMEM((ring - 1, 2, rows, width), BF16),
            pltpu.VMEM((ring - 1, 2, rows, narrow), BF16),
            pltpu.VMEM((ring - 1, 2, rows, wide), BF16),
            pltpu.VMEM((2, ring, rows, wide), BF16),
            pltpu.VMEM((rows, width), BF16),
            pltpu.VMEM((rows, narrow), BF16),
            pltpu.VMEM((rows, width), F32),
            pltpu.VMEM((4 * rows, quarter), F32),
            pltpu.SMEM((CAP, group), jnp.int32),
            pltpu.VMEM((mats + 1, rows, quarter), BF16),
            pltpu.VMEM((CAP, group, rows, quarter), BF16),
            pltpu.VMEM((CAP, group, rows, quarter), BF16),
            pltpu.VMEM((group * rows, quarter), BF16),
            pltpu.VMEM((CAP, group, rows, quarter), BF16),
            pltpu.VMEM((CAP, group, rows, quarter), BF16),
            dma((12,)),
            dma((ring - 1, 2)),
            dma((ring - 1, 2)),
            dma((ring - 1, 2)),
            dma((ring - 1, 2)),
            dma((ring - 1, 2)),
            dma((ring - 1, 2)),
            dma((ring, 2)),
            dma((ring, 2)),
            dma((2,)),
            dma((2,)),
            dma((CAP, group)),
            dma((CAP, group)),
            dma((CAP, group)),
            dma((CAP, group)),
        ],
        compiler_params=pltpu.CompilerParams(
            collective_id=0, has_side_effects=True, vmem_limit_bytes=56 * 2**20
        ),
    )(
        latent, query_grad, momentum.transpose(0, 2, 1, 3), by_row, gather, spread, split, join, owner_list
    )

    update = update.transpose(0, 2, 1, 3)
    step_scale = LEARN_RATE * RMS_FACTOR * math.sqrt(max(full_rows, width))
    clip_factor = jnp.minimum(1.0, CLIP_LIMIT / max_logit)
    row_index = lax.axis_index("dp") * rows_q + jnp.arange(rows_q)
    row_scale = jnp.where(
        row_index[None, None, :] < NOPE, jnp.sqrt(clip_factor)[:, :, None], clip_factor[:, :, None]
    )
    new_weight = (weight * (1.0 - LEARN_RATE * WEIGHT_DECAY) - step_scale * update) * row_scale[
        :, :, :, None
    ]
    return update, new_weight, new_momentum.transpose(0, 2, 1, 3), owned[None]


def solution(mesh):
    placed = (
        P(None, "dp", None),
        P(None, "dp", "expert"),
        P(None, "expert", "dp", None),
        P(None, "expert", "dp", None),
        P(None, "expert"),
        P(None, "expert"),
    )
    return jax.shard_map(
        on_device,
        mesh=mesh,
        in_specs=placed,
        out_specs=(
            P(None, "expert", "dp", None),
            P(None, "expert", "dp", None),
            P(None, "expert", "dp", None),
            P("expert", "dp", None, None),
        ),
        check_vma=False,
    )
```

```python
import functools
import math

import jax
import jax.numpy as jnp
import numpy as np
from jax import lax
from jax.experimental import pallas as pl
from jax.experimental.pallas import tpu as pltpu
from jax.sharding import PartitionSpec as P

NOPE = 128
CAP = 2
ITERS = 5
X_HI = 2

DECAY_RATE = 0.95
EPSILON = 1e-07
COEF_LINEAR = 3.4445
COEF_CUBIC = -4.775
COEF_QUINTIC = 2.0315
LEARN_RATE = 0.02
WEIGHT_DECAY = 0.1
CLIP_LIMIT = 100.0
RMS_FACTOR = 0.2

MESH = pl.DeviceIdType.MESH
F32 = jnp.float32
BF16 = jnp.bfloat16


def reorder_matrix(shape, axes):
    picked = np.arange(math.prod(shape)).reshape(shape).transpose(axes).reshape(-1)
    table = np.zeros((picked.size, picked.size), np.float32)
    table[np.arange(picked.size), picked] = 1.0
    return table


def remote(src, dst, send_sem, recv_sem, dp):
    return pltpu.make_async_remote_copy(
        src_ref=src,
        dst_ref=dst,
        send_sem=send_sem,
        recv_sem=recv_sem,
        device_id={"dp": dp},
        device_id_type=MESH,
    )


def full_dot(left, right):
    return jnp.dot(left, right, precision=lax.Precision.HIGHEST, preferred_element_type=F32)


def polynomial(gram):
    size = gram.shape[0]
    rows = lax.broadcasted_iota(jnp.int32, (size, size), 0)
    columns = lax.broadcasted_iota(jnp.int32, (size, size), 1)
    eye = jnp.where(rows == columns, 1.0, 0.0).astype(F32)
    total = None
    for sweep in range(ITERS):
        mixing = COEF_LINEAR * eye + COEF_CUBIC * gram + COEF_QUINTIC * full_dot(gram, gram)
        total = mixing if total is None else full_dot(mixing, total)
        if sweep < ITERS - 1:
            gram = full_dot(full_dot(mixing, gram), mixing)
    return total


def worker_of(mat, group):
    return 4 * (mat // 3) + (mat % 3 if mat % 3 < 2 else 2 + (mat // 3) % 2)


def orthogonalize(received, gather_ref, shuffled):
    shuffled[...] = jnp.dot(gather_ref[...], received, preferred_element_type=F32).astype(BF16)
    size = shuffled.shape[0] // 4
    gram = jnp.zeros((size, size), F32)
    for q in range(4):
        piece = shuffled[q * size : (q + 1) * size]
        gram = gram + lax.dot_general(
            piece, piece, (((1,), (1,)), ((), ())), preferred_element_type=F32
        )
    on_diagonal = lax.broadcasted_iota(jnp.int32, gram.shape, 0) == lax.broadcasted_iota(
        jnp.int32, gram.shape, 1
    )
    squares = jnp.sum(
        jnp.sum(jnp.where(on_diagonal, gram, 0.0), axis=1, keepdims=True), axis=0, keepdims=True
    )
    scale = 1.0 / (jnp.sqrt(squares) + EPSILON)
    mixed = polynomial(gram * scale * scale) * scale
    high = mixed.astype(BF16)
    low = (mixed - high.astype(F32)).astype(BF16)
    for q in range(4):
        span = slice(q * size, (q + 1) * size)
        piece = shuffled[span]
        shuffled[span] = (
            jnp.dot(high, piece, preferred_element_type=F32)
            + jnp.dot(low, piece, preferred_element_type=F32)
        ).astype(BF16)


def kernel(
    group,
    latent_hbm, grad_hbm, momentum_hbm, by_row_hbm, gather_hbm, spread_hbm, split_hbm, join_hbm, owner_ref,
    new_momentum_hbm, owned_hbm, update_hbm,
    new_momentum_ref, owned_ref, update_ref,
    latent_ref, grad_ref, momentum_ref, by_row_ref, gather_ref, spread_ref, split_ref, join_ref,
    cot, part_a, part_b, part_x, ring_a, ring_b, ring_x, cross_x, pair_a, pair_b,
    total, turned, pick, blocks, outgoing, incoming, shuffled, worked, back, returned,
    load_sem, send_a, got_a, send_b, got_b, send_x, got_x, send_c, got_c, send_p, got_p,
    send_out, got_out, send_work, got_work, send_back, got_back, store_sem,
):
    layers, rows_q, heads, width = momentum_ref.shape
    rows = heads * rows_q
    mats = layers * heads
    ring = group // X_HI
    quarter = width // 4
    half = width // 2
    narrow = part_b.shape[-1]
    extra = part_x.shape[-1] - half
    full_rows = rows_q * group
    me = lax.axis_index("dp")
    z = me // X_HI
    side = me % X_HI
    up = lax.rem(z + 1, ring) * X_HI + side
    down = lax.rem(z + ring - 1, ring) * X_HI + side
    partner = z * X_HI + 1 - side

    barrier = pltpu.get_barrier_semaphore()
    for peer in (up, down, partner):
        pl.semaphore_signal(barrier, inc=1, device_id={"dp": peer}, device_id_type=MESH)

    loads = {}
    for number, (name, src, dst) in enumerate(
        [
            ("by_row", by_row_hbm, by_row_ref),
            ("grad0", grad_hbm.at[0], grad_ref.at[0]),
            ("latent0", latent_hbm.at[0], latent_ref.at[0]),
            ("grad2", grad_hbm.at[2], grad_ref.at[2]),
            ("latent2", latent_hbm.at[2], latent_ref.at[2]),
            ("grad1", grad_hbm.at[1], grad_ref.at[1]),
            ("latent1", latent_hbm.at[1], latent_ref.at[1]),
            ("momentum", momentum_hbm, momentum_ref),
            ("split", split_hbm, split_ref),
            ("gather", gather_hbm, gather_ref),
            ("spread", spread_hbm, spread_ref),
            ("join", join_hbm, join_ref),
        ]
    ):
        loads[name] = pltpu.make_async_copy(src, dst, load_sem.at[number])
        loads[name].start()

    def products(layer, keep):
        loads["grad%d" % layer].wait()
        cot[...] = lax.dot_general(
            by_row_ref[...], grad_ref[layer], (((1,), (1,)), ((), ())), preferred_element_type=F32
        ).astype(BF16)
        loads["latent%d" % layer].wait()
        for first in range(0, group, 4):
            product = jnp.dot(
                cot[first * rows : (first + 4) * rows], latent_ref[layer], preferred_element_type=F32
            )
            keep(slice(first, first + 4), product.astype(BF16).reshape(4, rows, width))

    def keep_0(blocks_of, product):
        part_a[blocks_of] = product

    def keep_1(blocks_of, product):
        part_b[blocks_of] = product[:, :, :narrow]
        for way in range(2):
            begin = narrow + way * extra
            part_x[way, blocks_of, :, half:] = product[:, :, begin : begin + extra]

    def keep_2(blocks_of, product):
        for way in range(2):
            part_x[way, blocks_of, :, :half] = product[:, :, way * half : (way + 1) * half]

    def chunk_at(way, step):
        if way == 0:
            return lax.rem(z - 1 - step + 2 * ring, ring)
        return lax.rem(z + 1 + step, ring)

    def ring_copy(kind, way, step):
        chunk = chunk_at(way, step)
        src, dst, send, got = {
            "a": (part_a.at[chunk * X_HI + way], ring_a, send_a, got_a),
            "b": (part_b.at[chunk * X_HI + way], ring_b, send_b, got_b),
            "x": (part_x.at[way, chunk * X_HI + side], ring_x, send_x, got_x),
        }[kind]
        return remote(
            src, dst.at[step, way], send.at[step, way], got.at[step, way], up if way == 0 else down
        )

    def cross_copy(way, step):
        chunk = chunk_at(way, step)
        return remote(
            part_x.at[way, chunk * X_HI + 1 - side],
            cross_x.at[way, chunk],
            send_c.at[step, way],
            got_c.at[step, way],
            partner,
        )

    def pair_copy(kind):
        number, src, dst = {"a": (0, part_a, pair_a), "b": (1, part_b, pair_b)}[kind]
        return remote(src.at[partner], dst, send_p.at[number], got_p.at[number], partner)

    def ring_step(kind, way, step):
        if step >= 0:
            ring_copy(kind, way, step).wait_recv()
        if kind == "x":
            cross_copy(way, step + 1).wait_recv()
        if step == ring - 2:
            return
        chunk = chunk_at(way, step + 1)
        if kind == "x":
            spot = chunk * X_HI + side
            value = part_x[way, spot].astype(F32) + cross_x[way, chunk].astype(F32)
            if step >= 0:
                value = value + ring_x[step, way].astype(F32)
            part_x[way, spot] = value.astype(BF16)
        elif step >= 0:
            mine, came = {"a": (part_a, ring_a), "b": (part_b, ring_b)}[kind]
            spot = chunk * X_HI + way
            mine[spot] = (mine[spot].astype(F32) + came[step, way].astype(F32)).astype(BF16)
        ring_copy(kind, way, step + 1).start()

    def pair_step(kind):
        mine, came = {"a": (part_a, ring_a), "b": (part_b, ring_b)}[kind]
        mine[partner] = (
            mine[partner].astype(F32) + came[ring - 2, 1 - side].astype(F32)
        ).astype(BF16)
        pair_copy(kind).start()

    loads["by_row"].wait()
    products(0, keep_0)
    pl.semaphore_wait(barrier, 3)
    for way in range(2):
        ring_step("a", way, -1)
    products(2, keep_2)
    products(1, keep_1)
    for way in range(2):
        ring_step("b", way, -1)
    for step in range(3):
        for way in range(2):
            cross_copy(way, step).start()

    owner_of = [owner_ref[m // heads, m % heads] for m in range(mats)]
    slot_of = []
    for m in range(mats):
        slot = jnp.int32(0)
        for earlier in range(m):
            slot = slot + jnp.where(owner_of[earlier] == owner_of[m], 1, 0)
        slot_of.append(slot)

    @pl.loop(0, group)
    def _(owner):
        for slot in range(CAP):
            found = jnp.int32(mats)
            for m in range(mats):
                found = jnp.where((owner_of[m] == owner) & (slot_of[m] == slot), m, found)
            pick[slot, owner] = found

    for way in range(2):
        ring_step("a", way, 0)
    for way in range(2):
        ring_step("x", way, -1)
    for way in range(2):
        ring_step("b", way, 0)
    for step in range(1, ring - 1):
        if step + 2 < ring:
            for way in range(2):
                cross_copy(way, step + 2).start()
        for way in range(2):
            ring_step("a", way, step)
        if step == ring - 2:
            pair_step("a")
        for way in range(2):
            ring_step("x", way, step - 1)
        for way in range(2):
            ring_step("b", way, step)
        if step == ring - 2:
            pair_step("b")
    for way in range(2):
        ring_step("x", way, ring - 2)

    loads["momentum"].wait()
    loads["split"].wait()

    def last_sum(kind):
        mine, came, other = {"a": (part_a, ring_a, pair_a), "b": (part_b, ring_b, pair_b)}[kind]
        pair_copy(kind).wait_recv()
        return mine[me].astype(F32) + came[ring - 2, side].astype(F32) + other[...].astype(F32)

    def last_sum_x(way, columns):
        return (
            part_x[way, me, :, columns].astype(F32)
            + cross_x[way, z, :, columns].astype(F32)
            + ring_x[ring - 2, way, :, columns].astype(F32)
        )

    for layer in (2, 0, 1):
        if layer == 2:
            for way in range(2):
                total[:, way * half : (way + 1) * half] = last_sum_x(way, slice(0, half))
        elif layer == 0:
            total[...] = last_sum("a")
        else:
            total[:, :narrow] = last_sum("b")
            for way in range(2):
                begin = narrow + way * extra
                total[:, begin : begin + extra] = last_sum_x(way, slice(half, half + extra))
        for row in range(rows_q):
            span = slice(row * heads, (row + 1) * heads)
            fresh = DECAY_RATE * momentum_ref[layer, row] + total[span, :]
            new_momentum_ref[layer, row] = fresh
            total[span, :] = fresh
        stacked = jnp.concatenate(
            [total[:, q * quarter : (q + 1) * quarter].astype(BF16) for q in range(4)], axis=0
        )
        blocks[layer * heads : (layer + 1) * heads] = (
            jnp.dot(split_ref[...], stacked, preferred_element_type=F32)
            .astype(BF16)
            .reshape(heads, rows, quarter)
        )
    blocks[mats] = jnp.zeros((rows, quarter), BF16)

    stores = [pltpu.make_async_copy(new_momentum_ref, new_momentum_hbm, store_sem.at[0])]
    stores[0].start()

    def work_copy(mat):
        worker = worker_of(mat, group)
        return remote(blocks.at[mat], worked.at[me], send_work.at[mat], got_work.at[me], worker)

    def came_to_work(source):
        return remote(worked.at[source], worked.at[source], send_work.at[0], got_work.at[source], up)

    def back_copy(mat, step):
        peer = lax.rem(me + step, group)
        return remote(back.at[peer], returned.at[mat], send_back.at[step], got_back.at[mat], peer)

    def out_copy(slot, step):
        peer = lax.rem(me + step, group)
        return remote(
            outgoing.at[slot, peer],
            incoming.at[slot, me],
            send_out.at[slot, step],
            got_out.at[slot, step],
            peer,
        )

    for mat in range(mats):

        @pl.when(me != worker_of(mat, group))
        def _():
            work_copy(mat).start()

        @pl.when(me == worker_of(mat, group))
        def _():
            worked[me] = blocks[mat]

    for slot in range(CAP):

        @pl.loop(1, group)
        def _(step):
            peer = lax.rem(me + step, group)
            outgoing[slot, peer] = blocks[pick[slot, peer]]
            out_copy(slot, step).start()

        incoming[slot, me] = blocks[pick[slot, me]]

    loads["gather"].wait()
    loads["spread"].wait()
    loads["join"].wait()

    lot = me % 4
    works = (lot < 2) | (lot == 2 + (me // 4) % 2)
    mine = (me // 4) * 3 + jnp.minimum(lot, 2)

    @pl.when(works)
    def _():
        @pl.loop(1, group)
        def _(step):
            came_to_work(lax.rem(me + step, group)).wait_recv()

        orthogonalize(worked[...].reshape(group * rows, quarter), gather_ref, shuffled)
        back[...] = (
            jnp.dot(spread_ref[...], shuffled[...], preferred_element_type=F32)
            .astype(BF16)
            .reshape(group, rows, quarter)
        )

        @pl.loop(1, group)
        def _(step):
            back_copy(mine, step).start()

        returned[mine] = back[me]

    for slot in range(CAP):

        @pl.loop(1, group)
        def _(step):
            out_copy(slot, step).wait_recv()

        orthogonalize(incoming[slot].reshape(group * rows, quarter), gather_ref, shuffled)
        for q in range(4):
            owned_ref[slot, :, q * quarter : (q + 1) * quarter] = shuffled[
                q * full_rows : (q + 1) * full_rows
            ]
        stores.append(
            pltpu.make_async_copy(owned_ref.at[slot], owned_hbm.at[slot], store_sem.at[1 + slot])
        )
        stores[-1].start()

    for layer in range(layers):
        for head in range(heads):
            mat = layer * heads + head

            @pl.when(me != worker_of(mat, group))
            def _():
                back_copy(mat, 1).wait_recv()

        gathered = returned[layer * heads : (layer + 1) * heads].reshape(4 * rows, quarter)
        turned[...] = jnp.dot(join_ref[...], gathered, preferred_element_type=F32)
        for row in range(rows_q):
            for q in range(4):
                begin = q * rows + row * heads
                update_ref[layer, row, :, q * quarter : (q + 1) * quarter] = turned[
                    begin : begin + heads, :
                ]
        stores.append(
            pltpu.make_async_copy(
                update_ref.at[layer], update_hbm.at[layer], store_sem.at[1 + CAP + layer]
            )
        )
        stores[-1].start()

    for way in range(2):
        for step in range(ring - 1):
            for kind in "abx":
                ring_copy(kind, way, step).wait_send()
        for step in range(ring):
            cross_copy(way, step).wait_send()
    for kind in "ab":
        pair_copy(kind).wait_send()
    for mat in range(mats):

        @pl.when(me != worker_of(mat, group))
        def _():
            work_copy(mat).wait_send()

    @pl.when(works)
    def _():
        @pl.loop(1, group)
        def _(step):
            back_copy(mine, step).wait_send()

    for slot in range(CAP):

        @pl.loop(1, group)
        def _(step):
            out_copy(slot, step).wait_send()

    for store in stores:
        store.wait()


def finish(
    update_hbm, new_momentum_hbm, owned_hbm, weight_hbm, logit_ref,
    update_out, weight_out, new_momentum_out, owned_out,
    update, weight, new_weight, new_momentum, owned, load_sem, store_sem,
):
    layers, rows_q, heads, width = weight.shape
    full_rows = owned.shape[1]
    step_scale = LEARN_RATE * RMS_FACTOR * math.sqrt(max(full_rows, width))
    first_row = lax.axis_index("dp") * rows_q
    loads, stores = {}, {}
    for number, (name, src, via, dst) in enumerate(
        [
            ("update", update_hbm, update, update_out),
            ("weight", weight_hbm, weight, None),
            ("new_momentum", new_momentum_hbm, new_momentum, new_momentum_out),
            ("owned", owned_hbm, owned, owned_out),
        ]
    ):
        for part in range(via.shape[0]):
            loads[name, part] = pltpu.make_async_copy(
                src.at[part], via.at[part], load_sem.at[number, part]
            )
            loads[name, part].start()
            if dst is not None:
                stores[name, part] = pltpu.make_async_copy(
                    via.at[part], dst.at[part], store_sem.at[number, part]
                )
    on_diagonal = lax.broadcasted_iota(jnp.int32, (heads, heads), 0) == lax.broadcasted_iota(
        jnp.int32, (heads, heads), 1
    )
    for layer in range(layers):
        clip = jnp.minimum(1.0, CLIP_LIMIT / logit_ref[layer : layer + 1, :])
        clip = jnp.sum(
            jnp.where(on_diagonal, jnp.broadcast_to(clip, (heads, heads)), 0.0),
            axis=1,
            keepdims=True,
        )
        root = jnp.sqrt(clip)
        loads["update", layer].wait()
        stores["update", layer].start()
        loads["weight", layer].wait()
        for row in range(rows_q):
            scale = jnp.where(first_row + row < NOPE, root, clip)
            new_weight[layer, row] = (
                weight[layer, row] * (1.0 - LEARN_RATE * WEIGHT_DECAY)
                - step_scale * update[layer, row]
            ) * scale
        stores["weight", layer] = pltpu.make_async_copy(
            new_weight.at[layer], weight_out.at[layer], store_sem.at[1, layer]
        )
        stores["weight", layer].start()
    for name in ("new_momentum", "owned"):
        for part in range({"new_momentum": layers, "owned": CAP}[name]):
            loads[name, part].wait()
            stores[name, part].start()
    for store in stores.values():
        store.wait()


def on_device(latent, query_grad, momentum, weight, max_logit, owner_list):
    group = lax.axis_size("dp")
    layers, heads, rows_q, width = momentum.shape
    mats = layers * heads
    full_rows = rows_q * group
    rows = heads * rows_q
    quarter = width // 4
    half = width // 2
    ring = group // X_HI
    extra = width // 3
    narrow = width - 2 * extra
    wide = half + extra

    by_row = jnp.asarray(reorder_matrix((heads, group, rows_q), (1, 2, 0)), BF16)
    gather = jnp.asarray(reorder_matrix((group, 4, rows_q), (1, 0, 2)), BF16)
    spread = jnp.asarray(reorder_matrix((4, group, rows_q), (1, 0, 2)), BF16)
    split = jnp.asarray(reorder_matrix((4 * rows_q, heads), (1, 0)), BF16)
    join = jnp.asarray(reorder_matrix((heads, 4 * rows_q), (1, 0)), BF16)

    vmem = pl.BlockSpec(memory_space=pltpu.VMEM)
    smem = pl.BlockSpec(memory_space=pltpu.SMEM)
    hbm = pl.BlockSpec(memory_space=pl.ANY)
    by_rows = (layers, rows_q, heads, width)
    dma = pltpu.SemaphoreType.DMA
    new_momentum, owned, update = pl.pallas_call(
        functools.partial(kernel, group),
        out_shape=(
            jax.ShapeDtypeStruct(by_rows, F32),
            jax.ShapeDtypeStruct((CAP, full_rows, width), BF16),
            jax.ShapeDtypeStruct(by_rows, F32),
        ),
        in_specs=[hbm] * 8 + [smem],
        out_specs=(hbm, hbm, hbm),
        scratch_shapes=[
            pltpu.VMEM(by_rows, F32),
            pltpu.VMEM((CAP, full_rows, width), BF16),
            pltpu.VMEM(by_rows, F32),
            pltpu.VMEM(latent.shape, BF16),
            pltpu.VMEM(query_grad.shape, BF16),
            pltpu.VMEM(by_rows, F32),
            pltpu.VMEM(by_row.shape, BF16),
            pltpu.VMEM(gather.shape, BF16),
            pltpu.VMEM(spread.shape, BF16),
            pltpu.VMEM(split.shape, BF16),
            pltpu.VMEM(join.shape, BF16),
            pltpu.VMEM((heads * full_rows, latent.shape[1]), BF16),
            pltpu.VMEM((group, rows, width), BF16),
            pltpu.VMEM((group, rows, narrow), BF16),
            pltpu.VMEM((2, group, rows, wide), BF16),
            pltpu.VMEM((ring - 1, 2, rows, width), BF16),
            pltpu.VMEM((ring - 1, 2, rows, narrow), BF16),
            pltpu.VMEM((ring - 1, 2, rows, wide), BF16),
            pltpu.VMEM((2, ring, rows, wide), BF16),
            pltpu.VMEM((rows, width), BF16),
            pltpu.VMEM((rows, narrow), BF16),
            pltpu.VMEM((rows, width), F32),
            pltpu.VMEM((4 * rows, quarter), F32),
            pltpu.SMEM((CAP, group), jnp.int32),
            pltpu.VMEM((mats + 1, rows, quarter), BF16),
            pltpu.VMEM((CAP, group, rows, quarter), BF16),
            pltpu.VMEM((CAP, group, rows, quarter), BF16),
            pltpu.VMEM((group * rows, quarter), BF16),
            pltpu.VMEM((group, rows, quarter), BF16),
            pltpu.VMEM((group, rows, quarter), BF16),
            pltpu.VMEM((mats, rows, quarter), BF16),
            dma((12,)),
            dma((ring - 1, 2)),
            dma((ring - 1, 2)),
            dma((ring - 1, 2)),
            dma((ring - 1, 2)),
            dma((ring - 1, 2)),
            dma((ring - 1, 2)),
            dma((ring, 2)),
            dma((ring, 2)),
            dma((2,)),
            dma((2,)),
            dma((CAP, group)),
            dma((CAP, group)),
            dma((mats,)),
            dma((group,)),
            dma((group,)),
            dma((mats,)),
            dma((1 + CAP + layers,)),
        ],
        compiler_params=pltpu.CompilerParams(
            collective_id=0, has_side_effects=True, vmem_limit_bytes=56 * 2**20
        ),
    )(
        latent, query_grad, momentum.transpose(0, 2, 1, 3), by_row, gather, spread, split, join, owner_list
    )

    update, new_weight, new_momentum, owned = pl.pallas_call(
        finish,
        out_shape=(
            jax.ShapeDtypeStruct(by_rows, F32),
            jax.ShapeDtypeStruct(by_rows, F32),
            jax.ShapeDtypeStruct(by_rows, F32),
            jax.ShapeDtypeStruct((CAP, full_rows, width), BF16),
        ),
        in_specs=[hbm] * 4 + [vmem],
        out_specs=(hbm, hbm, hbm, hbm),
        scratch_shapes=[
            pltpu.VMEM(by_rows, F32),
            pltpu.VMEM(by_rows, F32),
            pltpu.VMEM(by_rows, F32),
            pltpu.VMEM(by_rows, F32),
            pltpu.VMEM((CAP, full_rows, width), BF16),
            dma((4, layers)),
            dma((4, layers)),
        ],
        compiler_params=pltpu.CompilerParams(vmem_limit_bytes=56 * 2**20),
    )(update, new_momentum, owned, weight.transpose(0, 2, 1, 3), max_logit)
    return (
        update.transpose(0, 2, 1, 3),
        new_weight.transpose(0, 2, 1, 3),
        new_momentum.transpose(0, 2, 1, 3),
        owned[None],
    )


def solution(mesh):
    placed = (
        P(None, "dp", None),
        P(None, "dp", "expert"),
        P(None, "expert", "dp", None),
        P(None, "expert", "dp", None),
        P(None, "expert"),
        P(None, "expert"),
    )
    return jax.shard_map(
        on_device,
        mesh=mesh,
        in_specs=placed,
        out_specs=(
            P(None, "expert", "dp", None),
            P(None, "expert", "dp", None),
            P(None, "expert", "dp", None),
            P("expert", "dp", None, None),
        ),
        check_vma=False,
    )
```

```python
import functools
import math

import jax
import jax.numpy as jnp
import numpy as np
from jax import lax
from jax.experimental import pallas as pl
from jax.experimental.pallas import tpu as pltpu
from jax.sharding import PartitionSpec as P

NOPE = 128
CAP = 2
ITERS = 5
X_HI = 2

DECAY_RATE = 0.95
EPSILON = 1e-07
COEF_LINEAR = 3.4445
COEF_CUBIC = -4.775
COEF_QUINTIC = 2.0315
LEARN_RATE = 0.02
WEIGHT_DECAY = 0.1
CLIP_LIMIT = 100.0
RMS_FACTOR = 0.2

MESH = pl.DeviceIdType.MESH
F32 = jnp.float32
BF16 = jnp.bfloat16


def reorder_matrix(shape, axes):
    picked = np.arange(math.prod(shape)).reshape(shape).transpose(axes).reshape(-1)
    table = np.zeros((picked.size, picked.size), np.float32)
    table[np.arange(picked.size), picked] = 1.0
    return table


def remote(src, dst, send_sem, recv_sem, dp):
    return pltpu.make_async_remote_copy(
        src_ref=src,
        dst_ref=dst,
        send_sem=send_sem,
        recv_sem=recv_sem,
        device_id={"dp": dp},
        device_id_type=MESH,
    )


def full_dot(left, right):
    return jnp.dot(left, right, precision=lax.Precision.HIGHEST, preferred_element_type=F32)


def polynomial(gram):
    size = gram.shape[0]
    rows = lax.broadcasted_iota(jnp.int32, (size, size), 0)
    columns = lax.broadcasted_iota(jnp.int32, (size, size), 1)
    eye = jnp.where(rows == columns, 1.0, 0.0).astype(F32)
    total = None
    for sweep in range(ITERS):
        mixing = COEF_LINEAR * eye + COEF_CUBIC * gram + COEF_QUINTIC * full_dot(gram, gram)
        total = mixing if total is None else full_dot(mixing, total)
        if sweep < ITERS - 1:
            gram = full_dot(full_dot(mixing, gram), mixing)
    return total


def worker_of(layer, head):
    return 4 * head + (layer if layer < 2 else 2 + head % 2)


def orthogonalize(received, gather_ref, shuffled):
    shuffled[...] = jnp.dot(gather_ref[...], received, preferred_element_type=F32).astype(BF16)
    size = shuffled.shape[0] // 4
    gram = jnp.zeros((size, size), F32)
    for q in range(4):
        piece = shuffled[q * size : (q + 1) * size]
        gram = gram + lax.dot_general(
            piece, piece, (((1,), (1,)), ((), ())), preferred_element_type=F32
        )
    on_diagonal = lax.broadcasted_iota(jnp.int32, gram.shape, 0) == lax.broadcasted_iota(
        jnp.int32, gram.shape, 1
    )
    squares = jnp.sum(
        jnp.sum(jnp.where(on_diagonal, gram, 0.0), axis=1, keepdims=True), axis=0, keepdims=True
    )
    scale = 1.0 / (jnp.sqrt(squares) + EPSILON)
    mixed = polynomial(gram * scale * scale) * scale
    high = mixed.astype(BF16)
    low = (mixed - high.astype(F32)).astype(BF16)
    for q in range(4):
        span = slice(q * size, (q + 1) * size)
        piece = shuffled[span]
        shuffled[span] = (
            jnp.dot(high, piece, preferred_element_type=F32)
            + jnp.dot(low, piece, preferred_element_type=F32)
        ).astype(BF16)


def kernel(
    group,
    latent_hbm, grad_hbm, momentum_hbm, by_row_hbm, gather_hbm, spread_hbm, split_hbm, join_hbm, owner_ref,
    new_momentum_hbm, owned_hbm, update_hbm,
    new_momentum_ref, owned_ref, update_ref,
    latent_ref, grad_ref, momentum_ref, by_row_ref, gather_ref, spread_ref, split_ref, join_ref,
    cot, part_a, part_b, part_x, ring_a, ring_b, ring_x, cross_x, pair_a, pair_b,
    total, turned, pick, blocks, outgoing, incoming, shuffled, worked, back, returned,
    load_sem, send_a, got_a, send_b, got_b, send_x, got_x, send_c, got_c, send_p, got_p,
    send_out, got_out, send_work, got_work, send_back, got_back, store_sem,
):
    layers, rows_q, heads, width = momentum_ref.shape
    rows = heads * rows_q
    mats = layers * heads
    ring = group // X_HI
    quarter = width // 4
    half = width // 2
    narrow = part_b.shape[-1]
    extra = part_x.shape[-1] - half
    full_rows = rows_q * group
    me = lax.axis_index("dp")
    z = me // X_HI
    side = me % X_HI
    up = lax.rem(z + 1, ring) * X_HI + side
    down = lax.rem(z + ring - 1, ring) * X_HI + side
    partner = z * X_HI + 1 - side

    barrier = pltpu.get_barrier_semaphore()
    for peer in (up, down, partner):
        pl.semaphore_signal(barrier, inc=1, device_id={"dp": peer}, device_id_type=MESH)

    loads = {}
    for number, (name, src, dst) in enumerate(
        [
            ("by_row", by_row_hbm, by_row_ref),
            ("grad0", grad_hbm.at[0], grad_ref.at[0]),
            ("latent0", latent_hbm.at[0], latent_ref.at[0]),
            ("grad2", grad_hbm.at[2], grad_ref.at[2]),
            ("latent2", latent_hbm.at[2], latent_ref.at[2]),
            ("grad1", grad_hbm.at[1], grad_ref.at[1]),
            ("latent1", latent_hbm.at[1], latent_ref.at[1]),
            ("momentum", momentum_hbm, momentum_ref),
            ("split", split_hbm, split_ref),
            ("gather", gather_hbm, gather_ref),
            ("spread", spread_hbm, spread_ref),
            ("join", join_hbm, join_ref),
        ]
    ):
        loads[name] = pltpu.make_async_copy(src, dst, load_sem.at[number])
        loads[name].start()

    def products(layer, keep):
        loads["grad%d" % layer].wait()
        cot[...] = lax.dot_general(
            by_row_ref[...], grad_ref[layer], (((1,), (1,)), ((), ())), preferred_element_type=F32
        ).astype(BF16)
        loads["latent%d" % layer].wait()
        for first in range(0, group, 4):
            product = jnp.dot(
                cot[first * rows : (first + 4) * rows], latent_ref[layer], preferred_element_type=F32
            )
            keep(slice(first, first + 4), product.astype(BF16).reshape(4, rows, width))

    def keep_0(blocks_of, product):
        part_a[blocks_of] = product

    def keep_1(blocks_of, product):
        part_b[blocks_of] = product[:, :, :narrow]
        for way in range(2):
            begin = narrow + way * extra
            part_x[way, blocks_of, :, half:] = product[:, :, begin : begin + extra]

    def keep_2(blocks_of, product):
        for way in range(2):
            part_x[way, blocks_of, :, :half] = product[:, :, way * half : (way + 1) * half]

    near, far = ring // 2 - 1, ring // 2

    def hops(way, lane):
        return far if way == lane else near

    def chunk_at(way, distance):
        if way == 0:
            return lax.rem(z + distance, ring)
        return lax.rem(z + ring - distance, ring)

    def ring_copy(kind, way, lane, step):
        chunk = chunk_at(way, hops(way, lane) - step)
        src, dst, send, got = {
            "a": (part_a.at[chunk * X_HI + lane], ring_a, send_a, got_a),
            "b": (part_b.at[chunk * X_HI + lane], ring_b, send_b, got_b),
            "x": (part_x.at[lane, chunk * X_HI + side], ring_x, send_x, got_x),
        }[kind]
        return remote(
            src,
            dst.at[step, way, lane],
            send.at[step, way, lane],
            got.at[step, way, lane],
            up if way == 0 else down,
        )

    cross_order = [(0, far)]
    for distance in range(near, 0, -1):
        cross_order += [(0, distance), (1, distance)]
    cross_order.append((0, 0))

    def cross_copy(place, lane):
        chunk = chunk_at(*cross_order[place])
        return remote(
            part_x.at[lane, chunk * X_HI + 1 - side],
            cross_x.at[lane, chunk],
            send_c.at[place, lane],
            got_c.at[place, lane],
            partner,
        )

    def pair_copy(kind):
        number, src, dst = {"a": (0, part_a, pair_a), "b": (1, part_b, pair_b)}[kind]
        return remote(src.at[partner], dst, send_p.at[number], got_p.at[number], partner)

    def cross(first, last):
        for place in range(first, last):
            for lane in range(2):
                cross_copy(place, lane).start()

    def ring_step(kind, way, lane, step):
        count = hops(way, lane)
        if step >= 0:
            ring_copy(kind, way, lane, step).wait_recv()
        if step == count - 1:
            return
        distance = count - step - 1
        chunk = chunk_at(way, distance)
        if kind == "x":
            place = cross_order.index((0 if distance == far else way, distance))
            cross_copy(place, lane).wait_recv()
            spot = chunk * X_HI + side
            value = part_x[lane, spot].astype(F32) + cross_x[lane, chunk].astype(F32)
            if step >= 0:
                value = value + ring_x[step, way, lane].astype(F32)
            part_x[lane, spot] = value.astype(BF16)
        elif step >= 0:
            mine, came = {"a": (part_a, ring_a), "b": (part_b, ring_b)}[kind]
            spot = chunk * X_HI + lane
            mine[spot] = (mine[spot].astype(F32) + came[step, way, lane].astype(F32)).astype(BF16)
        ring_copy(kind, way, lane, step + 1).start()

    def ring_far(kind, step):
        for way in range(2):
            ring_step(kind, way, way, step)

    def ring_near(kind, step):
        for way in range(2):
            ring_step(kind, way, 1 - way, step)

    def arrived(kind, lane):
        came = {"a": ring_a, "b": ring_b}[kind]
        if isinstance(lane, int):
            up_last, down_last = hops(0, lane) - 1, hops(1, lane) - 1
        else:
            up_last, down_last = far - 1 - lane, near - 1 + lane
        return came[up_last, 0, lane].astype(F32) + came[down_last, 1, lane].astype(F32)

    def pair_step(kind):
        mine = {"a": part_a, "b": part_b}[kind]
        mine[partner] = (mine[partner].astype(F32) + arrived(kind, 1 - side)).astype(BF16)
        pair_copy(kind).start()

    loads["by_row"].wait()
    products(0, keep_0)
    pl.semaphore_wait(barrier, 3)
    ring_far("a", -1)
    ring_near("a", -1)
    products(2, keep_2)
    products(1, keep_1)
    cross(0, 1)
    ring_far("b", -1)
    ring_near("b", -1)
    cross(1, 3)

    owner_of = [owner_ref[m // heads, m % heads] for m in range(mats)]
    slot_of = []
    for m in range(mats):
        slot = jnp.int32(0)
        for earlier in range(m):
            slot = slot + jnp.where(owner_of[earlier] == owner_of[m], 1, 0)
        slot_of.append(slot)

    @pl.loop(0, group)
    def _(owner):
        for slot in range(CAP):
            found = jnp.int32(mats)
            for m in range(mats):
                found = jnp.where((owner_of[m] == owner) & (slot_of[m] == slot), m, found)
            pick[slot, owner] = found

    ring_far("a", 0)
    ring_near("a", 0)
    ring_far("b", 0)
    ring_near("b", 0)
    ring_far("x", -1)
    cross(3, 5)
    ring_far("a", 1)
    ring_near("a", 1)
    ring_far("b", 1)
    ring_near("b", 1)
    ring_far("x", 0)
    ring_near("x", -1)
    cross(5, 7)
    ring_far("a", 2)
    ring_near("a", 2)
    ring_far("b", 2)
    ring_near("b", 2)
    ring_far("x", 1)
    ring_near("x", 0)
    cross(7, 8)
    ring_far("a", 3)
    pair_step("a")
    ring_far("b", 3)
    pair_step("b")
    ring_far("x", 2)
    ring_near("x", 1)
    ring_far("x", 3)
    ring_near("x", 2)
    for lane in range(2):
        cross_copy(ring - 1, lane).wait_recv()

    loads["momentum"].wait()
    loads["split"].wait()

    def last_sum(kind):
        mine, other = {"a": (part_a, pair_a), "b": (part_b, pair_b)}[kind]
        pair_copy(kind).wait_recv()
        return mine[me].astype(F32) + arrived(kind, side) + other[...].astype(F32)

    def last_sum_x(lane, columns):
        return (
            part_x[lane, me, :, columns].astype(F32)
            + cross_x[lane, z, :, columns].astype(F32)
            + ring_x[hops(0, lane) - 1, 0, lane, :, columns].astype(F32)
            + ring_x[hops(1, lane) - 1, 1, lane, :, columns].astype(F32)
        )

    def work_of(device):
        return jnp.minimum(device % 4, 2) * heads + device // 4

    def work_copy(layer, head):
        mat = layer * heads + head
        return remote(
            blocks.at[mat], worked.at[me], send_work.at[mat], got_work.at[me], worker_of(layer, head)
        )

    def work_from(source):
        return remote(worked.at[source], worked.at[source], send_work.at[0], got_work.at[source], up)

    lot = me % 4
    works = (lot < 2) | (lot == 2 + (me // 4) % 2)
    mine = work_of(me)

    for layer in (2, 0, 1):
        if layer == 2:
            for way in range(2):
                total[:, way * half : (way + 1) * half] = last_sum_x(way, slice(0, half))
        elif layer == 0:
            total[...] = last_sum("a")
        else:
            total[:, :narrow] = last_sum("b")
            for way in range(2):
                begin = narrow + way * extra
                total[:, begin : begin + extra] = last_sum_x(way, slice(half, half + extra))
        for row in range(rows_q):
            span = slice(row * heads, (row + 1) * heads)
            fresh = DECAY_RATE * momentum_ref[layer, row] + total[span, :]
            new_momentum_ref[layer, row] = fresh
            total[span, :] = fresh
        stacked = jnp.concatenate(
            [total[:, q * quarter : (q + 1) * quarter].astype(BF16) for q in range(4)], axis=0
        )
        blocks[layer * heads : (layer + 1) * heads] = (
            jnp.dot(split_ref[...], stacked, preferred_element_type=F32)
            .astype(BF16)
            .reshape(heads, rows, quarter)
        )
        for head in range(heads):

            @pl.when(me != worker_of(layer, head))
            def _():
                work_copy(layer, head).start()

    blocks[mats] = jnp.zeros((rows, quarter), BF16)

    stores = [pltpu.make_async_copy(new_momentum_ref, new_momentum_hbm, store_sem.at[0])]
    stores[0].start()

    def back_copy(mat, step):
        peer = lax.rem(me + step, group)
        return remote(back.at[peer], returned.at[mat], send_back.at[step], got_back.at[mat], peer)

    def out_copy(slot, step):
        peer = lax.rem(me + step, group)
        return remote(
            outgoing.at[slot, peer],
            incoming.at[slot, me],
            send_out.at[slot, step],
            got_out.at[slot, step],
            peer,
        )

    def send_slot(slot):
        @pl.loop(1, group)
        def _(step):
            peer = lax.rem(me + step, group)
            outgoing[slot, peer] = blocks[pick[slot, peer]]
            out_copy(slot, step).start()

        incoming[slot, me] = blocks[pick[slot, me]]

    def work_left():
        for layer in range(layers):
            for head in range(heads):

                @pl.when(me != worker_of(layer, head))
                def _():
                    work_copy(layer, head).wait_send()

    def slot_left(slot, first, last):
        @pl.loop(first, last)
        def _(step):
            out_copy(slot, step).wait_send()

    def do_work():
        @pl.when(works)
        def _():
            worked[me] = blocks[mine]

            @pl.loop(1, group)
            def _(step):
                work_from(lax.rem(me + step, group)).wait_recv()

            orthogonalize(worked[...].reshape(group * rows, quarter), gather_ref, shuffled)
            back[...] = (
                jnp.dot(spread_ref[...], shuffled[...], preferred_element_type=F32)
                .astype(BF16)
                .reshape(group, rows, quarter)
            )

    def post_back():
        @pl.when(works)
        def _():
            @pl.loop(1, group)
            def _(step):
                back_copy(mine, step).start()

            returned[mine] = back[me]

    loads["gather"].wait()
    loads["spread"].wait()
    loads["join"].wait()

    def own_slot(slot):
        @pl.loop(1, group)
        def _(step):
            out_copy(slot, step).wait_recv()

        orthogonalize(incoming[slot].reshape(group * rows, quarter), gather_ref, shuffled)
        for q in range(4):
            owned_ref[slot, :, q * quarter : (q + 1) * quarter] = shuffled[
                q * full_rows : (q + 1) * full_rows
            ]
        stores.append(
            pltpu.make_async_copy(owned_ref.at[slot], owned_hbm.at[slot], store_sem.at[1 + slot])
        )
        stores[-1].start()

    send_slot(0)
    work_left()
    send_slot(1)
    do_work()
    own_slot(0)
    slot_left(0, 1, group)
    slot_left(1, 1, group // 2)
    post_back()
    own_slot(1)
    slot_left(1, group // 2, group)

    for layer in range(layers):
        for head in range(heads):
            mat = layer * heads + head

            @pl.when(me != worker_of(layer, head))
            def _():
                back_copy(mat, 1).wait_recv()

        gathered = returned[layer * heads : (layer + 1) * heads].reshape(4 * rows, quarter)
        turned[...] = jnp.dot(join_ref[...], gathered, preferred_element_type=F32)
        for row in range(rows_q):
            for q in range(4):
                begin = q * rows + row * heads
                update_ref[layer, row, :, q * quarter : (q + 1) * quarter] = turned[
                    begin : begin + heads, :
                ]
        stores.append(
            pltpu.make_async_copy(
                update_ref.at[layer], update_hbm.at[layer], store_sem.at[1 + CAP + layer]
            )
        )
        stores[-1].start()

    for kind in "abx":
        for way in range(2):
            for lane in range(2):
                for step in range(hops(way, lane)):
                    ring_copy(kind, way, lane, step).wait_send()
    for place in range(ring):
        for lane in range(2):
            cross_copy(place, lane).wait_send()
    for kind in "ab":
        pair_copy(kind).wait_send()
    @pl.when(works)
    def _():
        @pl.loop(1, group)
        def _(step):
            back_copy(mine, step).wait_send()

    for store in stores:
        store.wait()


def finish(
    update_hbm, new_momentum_hbm, owned_hbm, weight_hbm, logit_ref,
    update_out, weight_out, new_momentum_out, owned_out,
    update, weight, new_weight, new_momentum, owned, load_sem, store_sem,
):
    layers, rows_q, heads, width = weight.shape
    full_rows = owned.shape[1]
    step_scale = LEARN_RATE * RMS_FACTOR * math.sqrt(max(full_rows, width))
    first_row = lax.axis_index("dp") * rows_q
    loads, stores = {}, {}
    for number, (name, src, via, dst) in enumerate(
        [
            ("update", update_hbm, update, update_out),
            ("weight", weight_hbm, weight, None),
            ("new_momentum", new_momentum_hbm, new_momentum, new_momentum_out),
            ("owned", owned_hbm, owned, owned_out),
        ]
    ):
        for part in range(via.shape[0]):
            loads[name, part] = pltpu.make_async_copy(
                src.at[part], via.at[part], load_sem.at[number, part]
            )
            loads[name, part].start()
            if dst is not None:
                stores[name, part] = pltpu.make_async_copy(
                    via.at[part], dst.at[part], store_sem.at[number, part]
                )
    on_diagonal = lax.broadcasted_iota(jnp.int32, (heads, heads), 0) == lax.broadcasted_iota(
        jnp.int32, (heads, heads), 1
    )
    for layer in range(layers):
        clip = jnp.minimum(1.0, CLIP_LIMIT / logit_ref[layer : layer + 1, :])
        clip = jnp.sum(
            jnp.where(on_diagonal, jnp.broadcast_to(clip, (heads, heads)), 0.0),
            axis=1,
            keepdims=True,
        )
        root = jnp.sqrt(clip)
        loads["update", layer].wait()
        stores["update", layer].start()
        loads["weight", layer].wait()
        for row in range(rows_q):
            scale = jnp.where(first_row + row < NOPE, root, clip)
            new_weight[layer, row] = (
                weight[layer, row] * (1.0 - LEARN_RATE * WEIGHT_DECAY)
                - step_scale * update[layer, row]
            ) * scale
        stores["weight", layer] = pltpu.make_async_copy(
            new_weight.at[layer], weight_out.at[layer], store_sem.at[1, layer]
        )
        stores["weight", layer].start()
    for name in ("new_momentum", "owned"):
        for part in range({"new_momentum": layers, "owned": CAP}[name]):
            loads[name, part].wait()
            stores[name, part].start()
    for store in stores.values():
        store.wait()


def on_device(latent, query_grad, momentum, weight, max_logit, owner_list):
    group = lax.axis_size("dp")
    layers, heads, rows_q, width = momentum.shape
    mats = layers * heads
    full_rows = rows_q * group
    rows = heads * rows_q
    quarter = width // 4
    half = width // 2
    ring = group // X_HI
    extra = width // 3
    narrow = width - 2 * extra
    wide = half + extra

    by_row = jnp.asarray(reorder_matrix((heads, group, rows_q), (1, 2, 0)), BF16)
    gather = jnp.asarray(reorder_matrix((group, 4, rows_q), (1, 0, 2)), BF16)
    spread = jnp.asarray(reorder_matrix((4, group, rows_q), (1, 0, 2)), BF16)
    split = jnp.asarray(reorder_matrix((4 * rows_q, heads), (1, 0)), BF16)
    join = jnp.asarray(reorder_matrix((heads, 4 * rows_q), (1, 0)), BF16)

    vmem = pl.BlockSpec(memory_space=pltpu.VMEM)
    smem = pl.BlockSpec(memory_space=pltpu.SMEM)
    hbm = pl.BlockSpec(memory_space=pl.ANY)
    by_rows = (layers, rows_q, heads, width)
    dma = pltpu.SemaphoreType.DMA
    new_momentum, owned, update = pl.pallas_call(
        functools.partial(kernel, group),
        out_shape=(
            jax.ShapeDtypeStruct(by_rows, F32),
            jax.ShapeDtypeStruct((CAP, full_rows, width), BF16),
            jax.ShapeDtypeStruct(by_rows, F32),
        ),
        in_specs=[hbm] * 8 + [smem],
        out_specs=(hbm, hbm, hbm),
        scratch_shapes=[
            pltpu.VMEM(by_rows, F32),
            pltpu.VMEM((CAP, full_rows, width), BF16),
            pltpu.VMEM(by_rows, F32),
            pltpu.VMEM(latent.shape, BF16),
            pltpu.VMEM(query_grad.shape, BF16),
            pltpu.VMEM(by_rows, F32),
            pltpu.VMEM(by_row.shape, BF16),
            pltpu.VMEM(gather.shape, BF16),
            pltpu.VMEM(spread.shape, BF16),
            pltpu.VMEM(split.shape, BF16),
            pltpu.VMEM(join.shape, BF16),
            pltpu.VMEM((heads * full_rows, latent.shape[1]), BF16),
            pltpu.VMEM((group, rows, width), BF16),
            pltpu.VMEM((group, rows, narrow), BF16),
            pltpu.VMEM((2, group, rows, wide), BF16),
            pltpu.VMEM((ring // 2, 2, 2, rows, width), BF16),
            pltpu.VMEM((ring // 2, 2, 2, rows, narrow), BF16),
            pltpu.VMEM((ring // 2, 2, 2, rows, wide), BF16),
            pltpu.VMEM((2, ring, rows, wide), BF16),
            pltpu.VMEM((rows, width), BF16),
            pltpu.VMEM((rows, narrow), BF16),
            pltpu.VMEM((rows, width), F32),
            pltpu.VMEM((4 * rows, quarter), F32),
            pltpu.SMEM((CAP, group), jnp.int32),
            pltpu.VMEM((mats + 1, rows, quarter), BF16),
            pltpu.VMEM((CAP, group, rows, quarter), BF16),
            pltpu.VMEM((CAP, group, rows, quarter), BF16),
            pltpu.VMEM((group * rows, quarter), BF16),
            pltpu.VMEM((group, rows, quarter), BF16),
            pltpu.VMEM((group, rows, quarter), BF16),
            pltpu.VMEM((mats, rows, quarter), BF16),
            dma((12,)),
            dma((ring // 2, 2, 2)),
            dma((ring // 2, 2, 2)),
            dma((ring // 2, 2, 2)),
            dma((ring // 2, 2, 2)),
            dma((ring // 2, 2, 2)),
            dma((ring // 2, 2, 2)),
            dma((ring, 2)),
            dma((ring, 2)),
            dma((2,)),
            dma((2,)),
            dma((CAP, group)),
            dma((CAP, group)),
            dma((mats,)),
            dma((group,)),
            dma((group,)),
            dma((mats,)),
            dma((1 + CAP + layers,)),
        ],
        compiler_params=pltpu.CompilerParams(
            collective_id=0, has_side_effects=True, vmem_limit_bytes=56 * 2**20
        ),
    )(
        latent, query_grad, momentum.transpose(0, 2, 1, 3), by_row, gather, spread, split, join, owner_list
    )

    update, new_weight, new_momentum, owned = pl.pallas_call(
        finish,
        out_shape=(
            jax.ShapeDtypeStruct(by_rows, F32),
            jax.ShapeDtypeStruct(by_rows, F32),
            jax.ShapeDtypeStruct(by_rows, F32),
            jax.ShapeDtypeStruct((CAP, full_rows, width), BF16),
        ),
        in_specs=[hbm] * 4 + [vmem],
        out_specs=(hbm, hbm, hbm, hbm),
        scratch_shapes=[
            pltpu.VMEM(by_rows, F32),
            pltpu.VMEM(by_rows, F32),
            pltpu.VMEM(by_rows, F32),
            pltpu.VMEM(by_rows, F32),
            pltpu.VMEM((CAP, full_rows, width), BF16),
            dma((4, layers)),
            dma((4, layers)),
        ],
        compiler_params=pltpu.CompilerParams(vmem_limit_bytes=56 * 2**20),
    )(update, new_momentum, owned, weight.transpose(0, 2, 1, 3), max_logit)
    return (
        update.transpose(0, 2, 1, 3),
        new_weight.transpose(0, 2, 1, 3),
        new_momentum.transpose(0, 2, 1, 3),
        owned[None],
    )


def solution(mesh):
    placed = (
        P(None, "dp", None),
        P(None, "dp", "expert"),
        P(None, "expert", "dp", None),
        P(None, "expert", "dp", None),
        P(None, "expert"),
        P(None, "expert"),
    )
    return jax.shard_map(
        on_device,
        mesh=mesh,
        in_specs=placed,
        out_specs=(
            P(None, "expert", "dp", None),
            P(None, "expert", "dp", None),
            P(None, "expert", "dp", None),
            P("expert", "dp", None, None),
        ),
        check_vma=False,
    )
```

```python
import functools
import math

import jax
import jax.numpy as jnp
import numpy as np
from jax import lax
from jax.experimental import pallas as pl
from jax.experimental.pallas import tpu as pltpu
from jax.sharding import PartitionSpec as P

NOPE = 128
CAP = 2
ITERS = 5
X_HI = 2

DECAY_RATE = 0.95
EPSILON = 1e-07
COEF_LINEAR = 3.4445
COEF_CUBIC = -4.775
COEF_QUINTIC = 2.0315
LEARN_RATE = 0.02
WEIGHT_DECAY = 0.1
CLIP_LIMIT = 100.0
RMS_FACTOR = 0.2

MESH = pl.DeviceIdType.MESH
F32 = jnp.float32
BF16 = jnp.bfloat16


def reorder_matrix(shape, axes):
    picked = np.arange(math.prod(shape)).reshape(shape).transpose(axes).reshape(-1)
    table = np.zeros((picked.size, picked.size), np.float32)
    table[np.arange(picked.size), picked] = 1.0
    return table


def remote(src, dst, send_sem, recv_sem, dp):
    return pltpu.make_async_remote_copy(
        src_ref=src,
        dst_ref=dst,
        send_sem=send_sem,
        recv_sem=recv_sem,
        device_id={"dp": dp},
        device_id_type=MESH,
    )


def parts_of(value, count):
    parts = []
    for _ in range(count):
        parts.append(value.astype(BF16))
        value = value - parts[-1].astype(F32)
    return parts


def part_dot(left, right):
    size = left[0].shape[0]
    count = len(right)
    result = None
    for place in range(count - 1, -1, -1):
        stacked = left[0] if place == count - 1 else jnp.concatenate(left[: count - place], axis=0)
        product = jnp.dot(stacked, right[place], preferred_element_type=F32)
        for row in range(count - place - 1, -1, -1):
            term = product[row * size : (row + 1) * size]
            result = term if result is None else result + term
    return result


def polynomial(gram):
    size = gram.shape[0]
    rows = lax.broadcasted_iota(jnp.int32, (size, size), 0)
    columns = lax.broadcasted_iota(jnp.int32, (size, size), 1)
    eye = jnp.where(rows == columns, 1.0, 0.0).astype(F32)
    total = None
    for sweep in range(ITERS):
        count = 3 if sweep < 3 else 2
        gram_parts = parts_of(gram, count)
        mixing = (
            COEF_LINEAR * eye + COEF_CUBIC * gram + COEF_QUINTIC * part_dot(gram_parts, gram_parts)
        )
        mixing_parts = parts_of(mixing, count)
        if sweep < ITERS - 1:
            gram = part_dot(parts_of(part_dot(mixing_parts, gram_parts), count), mixing_parts)
        total = mixing if total is None else part_dot(parts_of(total, 2), mixing_parts[:2])
    return total


def worker_of(layer, head):
    return 4 * head + (layer if layer < 2 else 2 + head % 2)


def orthogonalize(received, gather_ref, shuffled):
    shuffled[...] = jnp.dot(gather_ref[...], received, preferred_element_type=F32).astype(BF16)
    size = shuffled.shape[0] // 4
    gram = jnp.zeros((size, size), F32)
    for q in range(4):
        piece = shuffled[q * size : (q + 1) * size]
        gram = gram + lax.dot_general(
            piece, piece, (((1,), (1,)), ((), ())), preferred_element_type=F32
        )
    on_diagonal = lax.broadcasted_iota(jnp.int32, gram.shape, 0) == lax.broadcasted_iota(
        jnp.int32, gram.shape, 1
    )
    squares = jnp.sum(
        jnp.sum(jnp.where(on_diagonal, gram, 0.0), axis=1, keepdims=True), axis=0, keepdims=True
    )
    scale = 1.0 / (jnp.sqrt(squares) + EPSILON)
    mixed = polynomial(gram * scale * scale) * scale
    high = mixed.astype(BF16)
    low = (mixed - high.astype(F32)).astype(BF16)
    for q in range(4):
        span = slice(q * size, (q + 1) * size)
        piece = shuffled[span]
        shuffled[span] = (
            jnp.dot(high, piece, preferred_element_type=F32)
            + jnp.dot(low, piece, preferred_element_type=F32)
        ).astype(BF16)


def kernel(
    group,
    latent_hbm, grad_hbm, momentum_hbm, weight_hbm, by_row_hbm, gather_hbm, spread_hbm, split_hbm, join_hbm,
    logit_ref, owner_ref,
    new_momentum_ref, owned_ref, update_ref, new_weight_ref,
    weight_ref,
    latent_ref, grad_ref, momentum_ref, by_row_ref, gather_ref, spread_ref, split_ref, join_ref,
    cot, part_a, part_b, part_x, ring_a, ring_b, ring_x, cross_x, pair_a, pair_b,
    total, turned, pick, blocks, outgoing, incoming, shuffled, worked, back, returned,
    load_sem, send_a, got_a, send_b, got_b, send_x, got_x, send_c, got_c, send_p, got_p,
    send_out, got_out, send_work, got_work, send_back, got_back,
):
    layers, rows_q, heads, width = momentum_ref.shape
    rows = heads * rows_q
    mats = layers * heads
    ring = group // X_HI
    quarter = width // 4
    half = width // 2
    narrow = part_b.shape[-1]
    extra = part_x.shape[-1] - half
    full_rows = rows_q * group
    me = lax.axis_index("dp")
    z = me // X_HI
    side = me % X_HI
    up = lax.rem(z + 1, ring) * X_HI + side
    down = lax.rem(z + ring - 1, ring) * X_HI + side
    partner = z * X_HI + 1 - side

    barrier = pltpu.get_barrier_semaphore()
    for peer in (up, down, partner):
        pl.semaphore_signal(barrier, inc=1, device_id={"dp": peer}, device_id_type=MESH)

    loads = {}
    for number, (name, src, dst) in enumerate(
        [
            ("by_row", by_row_hbm, by_row_ref),
            ("grad0", grad_hbm.at[0], grad_ref.at[0]),
            ("latent0", latent_hbm.at[0], latent_ref.at[0]),
            ("grad2", grad_hbm.at[2], grad_ref.at[2]),
            ("latent2", latent_hbm.at[2], latent_ref.at[2]),
            ("grad1", grad_hbm.at[1], grad_ref.at[1]),
            ("latent1", latent_hbm.at[1], latent_ref.at[1]),
            ("momentum", momentum_hbm, momentum_ref),
            ("split", split_hbm, split_ref),
            ("gather", gather_hbm, gather_ref),
            ("spread", spread_hbm, spread_ref),
            ("join", join_hbm, join_ref),
            ("weight", weight_hbm, weight_ref),
        ]
    ):
        loads[name] = pltpu.make_async_copy(src, dst, load_sem.at[number])
        loads[name].start()

    def products(layer, keep):
        loads["grad%d" % layer].wait()
        cot[...] = lax.dot_general(
            by_row_ref[...], grad_ref[layer], (((1,), (1,)), ((), ())), preferred_element_type=F32
        ).astype(BF16)
        loads["latent%d" % layer].wait()
        for first in range(0, group, 4):
            product = jnp.dot(
                cot[first * rows : (first + 4) * rows], latent_ref[layer], preferred_element_type=F32
            )
            keep(slice(first, first + 4), product.astype(BF16).reshape(4, rows, width))

    def keep_0(blocks_of, product):
        part_a[blocks_of] = product

    def keep_1(blocks_of, product):
        part_b[blocks_of] = product[:, :, :narrow]
        for way in range(2):
            begin = narrow + way * extra
            part_x[way, blocks_of, :, half:] = product[:, :, begin : begin + extra]

    def keep_2(blocks_of, product):
        for way in range(2):
            part_x[way, blocks_of, :, :half] = product[:, :, way * half : (way + 1) * half]

    near, far = ring // 2 - 1, ring // 2

    def hops(way, lane):
        return far if way == lane else near

    def chunk_at(way, distance):
        if way == 0:
            return lax.rem(z + distance, ring)
        return lax.rem(z + ring - distance, ring)

    def ring_copy(kind, way, lane, step):
        chunk = chunk_at(way, hops(way, lane) - step)
        src, dst, send, got = {
            "a": (part_a.at[chunk * X_HI + lane], ring_a, send_a, got_a),
            "b": (part_b.at[chunk * X_HI + lane], ring_b, send_b, got_b),
            "x": (part_x.at[lane, chunk * X_HI + side], ring_x, send_x, got_x),
        }[kind]
        return remote(
            src,
            dst.at[step, way, lane],
            send.at[step, way, lane],
            got.at[step, way, lane],
            up if way == 0 else down,
        )

    cross_order = [(0, far)]
    for distance in range(near, 0, -1):
        cross_order += [(0, distance), (1, distance)]
    cross_order.append((0, 0))

    def cross_copy(place, lane):
        chunk = chunk_at(*cross_order[place])
        return remote(
            part_x.at[lane, chunk * X_HI + 1 - side],
            cross_x.at[lane, chunk],
            send_c.at[place, lane],
            got_c.at[place, lane],
            partner,
        )

    def pair_copy(kind):
        number, src, dst = {"a": (0, part_a, pair_a), "b": (1, part_b, pair_b)}[kind]
        return remote(src.at[partner], dst, send_p.at[number], got_p.at[number], partner)

    def cross(first, last):
        for place in range(first, last):
            for lane in range(2):
                cross_copy(place, lane).start()

    def ring_step(kind, way, lane, step):
        count = hops(way, lane)
        if step >= 0:
            ring_copy(kind, way, lane, step).wait_recv()
        if step == count - 1:
            return
        distance = count - step - 1
        chunk = chunk_at(way, distance)
        if kind == "x":
            place = cross_order.index((0 if distance == far else way, distance))
            cross_copy(place, lane).wait_recv()
            spot = chunk * X_HI + side
            value = part_x[lane, spot].astype(F32) + cross_x[lane, chunk].astype(F32)
            if step >= 0:
                value = value + ring_x[step, way, lane].astype(F32)
            part_x[lane, spot] = value.astype(BF16)
        elif step >= 0:
            mine, came = {"a": (part_a, ring_a), "b": (part_b, ring_b)}[kind]
            spot = chunk * X_HI + lane
            mine[spot] = (mine[spot].astype(F32) + came[step, way, lane].astype(F32)).astype(BF16)
        ring_copy(kind, way, lane, step + 1).start()

    def ring_far(kind, step):
        for way in range(2):
            ring_step(kind, way, way, step)

    def ring_near(kind, step):
        for way in range(2):
            ring_step(kind, way, 1 - way, step)

    def arrived(kind, lane):
        came = {"a": ring_a, "b": ring_b}[kind]
        if isinstance(lane, int):
            up_last, down_last = hops(0, lane) - 1, hops(1, lane) - 1
        else:
            up_last, down_last = far - 1 - lane, near - 1 + lane
        return came[up_last, 0, lane].astype(F32) + came[down_last, 1, lane].astype(F32)

    def pair_step(kind):
        mine = {"a": part_a, "b": part_b}[kind]
        mine[partner] = (mine[partner].astype(F32) + arrived(kind, 1 - side)).astype(BF16)
        pair_copy(kind).start()

    loads["by_row"].wait()
    products(0, keep_0)
    pl.semaphore_wait(barrier, 3)
    ring_far("a", -1)
    ring_near("a", -1)
    products(2, keep_2)
    products(1, keep_1)
    cross(0, 1)
    ring_far("b", -1)
    ring_near("b", -1)
    cross(1, 3)

    owner_of = [owner_ref[m // heads, m % heads] for m in range(mats)]
    slot_of = []
    for m in range(mats):
        slot = jnp.int32(0)
        for earlier in range(m):
            slot = slot + jnp.where(owner_of[earlier] == owner_of[m], 1, 0)
        slot_of.append(slot)

    @pl.loop(0, group)
    def _(owner):
        for slot in range(CAP):
            found = jnp.int32(mats)
            for m in range(mats):
                found = jnp.where((owner_of[m] == owner) & (slot_of[m] == slot), m, found)
            pick[slot, owner] = found

    ring_far("a", 0)
    ring_near("a", 0)
    ring_far("b", 0)
    ring_near("b", 0)
    ring_far("x", -1)
    cross(3, 5)
    ring_far("a", 1)
    ring_near("a", 1)
    ring_far("b", 1)
    ring_near("b", 1)
    ring_far("x", 0)
    ring_near("x", -1)
    cross(5, 7)
    ring_far("a", 2)
    ring_near("a", 2)
    ring_far("b", 2)
    ring_near("b", 2)
    ring_far("x", 1)
    ring_near("x", 0)
    cross(7, 8)
    ring_far("a", 3)
    pair_step("a")
    ring_far("b", 3)
    pair_step("b")
    ring_far("x", 2)
    ring_near("x", 1)
    ring_far("x", 3)
    ring_near("x", 2)
    for lane in range(2):
        cross_copy(ring - 1, lane).wait_recv()

    loads["momentum"].wait()
    loads["split"].wait()

    def last_sum(kind):
        mine, other = {"a": (part_a, pair_a), "b": (part_b, pair_b)}[kind]
        pair_copy(kind).wait_recv()
        return mine[me].astype(F32) + arrived(kind, side) + other[...].astype(F32)

    def last_sum_x(lane, columns):
        return (
            part_x[lane, me, :, columns].astype(F32)
            + cross_x[lane, z, :, columns].astype(F32)
            + ring_x[hops(0, lane) - 1, 0, lane, :, columns].astype(F32)
            + ring_x[hops(1, lane) - 1, 1, lane, :, columns].astype(F32)
        )

    def work_of(device):
        return jnp.minimum(device % 4, 2) * heads + device // 4

    def work_copy(layer, head):
        mat = layer * heads + head
        return remote(
            blocks.at[mat], worked.at[me], send_work.at[mat], got_work.at[me], worker_of(layer, head)
        )

    def work_from(source):
        return remote(worked.at[source], worked.at[source], send_work.at[0], got_work.at[source], up)

    lot = me % 4
    works = (lot < 2) | (lot == 2 + (me // 4) % 2)
    mine = work_of(me)

    for layer in (2, 0, 1):
        if layer == 2:
            for way in range(2):
                total[:, way * half : (way + 1) * half] = last_sum_x(way, slice(0, half))
        elif layer == 0:
            total[...] = last_sum("a")
        else:
            total[:, :narrow] = last_sum("b")
            for way in range(2):
                begin = narrow + way * extra
                total[:, begin : begin + extra] = last_sum_x(way, slice(half, half + extra))
        for row in range(rows_q):
            span = slice(row * heads, (row + 1) * heads)
            fresh = DECAY_RATE * momentum_ref[layer, row] + total[span, :]
            new_momentum_ref[layer, row] = fresh
            total[span, :] = fresh
        stacked = jnp.concatenate(
            [total[:, q * quarter : (q + 1) * quarter].astype(BF16) for q in range(4)], axis=0
        )
        blocks[layer * heads : (layer + 1) * heads] = (
            jnp.dot(split_ref[...], stacked, preferred_element_type=F32)
            .astype(BF16)
            .reshape(heads, rows, quarter)
        )
        for head in range(heads):

            @pl.when(me != worker_of(layer, head))
            def _():
                work_copy(layer, head).start()

    blocks[mats] = jnp.zeros((rows, quarter), BF16)


    def back_copy(mat, step):
        peer = lax.rem(me + step, group)
        return remote(back.at[peer], returned.at[mat], send_back.at[step], got_back.at[mat], peer)

    def out_copy(slot, step):
        peer = lax.rem(me + step, group)
        return remote(
            outgoing.at[slot, peer],
            incoming.at[slot, me],
            send_out.at[slot, step],
            got_out.at[slot, step],
            peer,
        )

    def send_slot(slot):
        @pl.loop(1, group)
        def _(step):
            peer = lax.rem(me + step, group)
            outgoing[slot, peer] = blocks[pick[slot, peer]]
            out_copy(slot, step).start()

        incoming[slot, me] = blocks[pick[slot, me]]

    def work_left():
        for layer in range(layers):
            for head in range(heads):

                @pl.when(me != worker_of(layer, head))
                def _():
                    work_copy(layer, head).wait_send()

    def slot_left(slot, first, last):
        @pl.loop(first, last)
        def _(step):
            out_copy(slot, step).wait_send()

    def do_work():
        @pl.when(works)
        def _():
            worked[me] = blocks[mine]

            @pl.loop(1, group)
            def _(step):
                work_from(lax.rem(me + step, group)).wait_recv()

            orthogonalize(worked[...].reshape(group * rows, quarter), gather_ref, shuffled)
            back[...] = (
                jnp.dot(spread_ref[...], shuffled[...], preferred_element_type=F32)
                .astype(BF16)
                .reshape(group, rows, quarter)
            )

    def post_back():
        @pl.when(works)
        def _():
            @pl.loop(1, group)
            def _(step):
                back_copy(mine, step).start()

            returned[mine] = back[me]

    loads["gather"].wait()
    loads["spread"].wait()
    loads["join"].wait()

    def own_slot(slot):
        @pl.loop(1, group)
        def _(step):
            out_copy(slot, step).wait_recv()

        orthogonalize(incoming[slot].reshape(group * rows, quarter), gather_ref, shuffled)
        for q in range(4):
            owned_ref[slot, :, q * quarter : (q + 1) * quarter] = shuffled[
                q * full_rows : (q + 1) * full_rows
            ]

    send_slot(0)
    work_left()
    send_slot(1)
    do_work()
    own_slot(0)
    slot_left(0, 1, group)
    slot_left(1, 1, group)
    post_back()
    own_slot(1)

    loads["weight"].wait()
    step_scale = LEARN_RATE * RMS_FACTOR * math.sqrt(max(full_rows, width))
    heads_diagonal = lax.broadcasted_iota(jnp.int32, (heads, heads), 0) == lax.broadcasted_iota(
        jnp.int32, (heads, heads), 1
    )
    for layer in range(layers):
        for head in range(heads):
            mat = layer * heads + head

            @pl.when(me != worker_of(layer, head))
            def _():
                back_copy(mat, 1).wait_recv()

        gathered = returned[layer * heads : (layer + 1) * heads].reshape(4 * rows, quarter)
        turned[...] = jnp.dot(join_ref[...], gathered, preferred_element_type=F32)
        clip = jnp.minimum(1.0, CLIP_LIMIT / logit_ref[layer : layer + 1, :])
        clip = jnp.sum(
            jnp.where(heads_diagonal, jnp.broadcast_to(clip, (heads, heads)), 0.0),
            axis=1,
            keepdims=True,
        )
        root = jnp.sqrt(clip)
        for row in range(rows_q):
            scale = jnp.where(me * rows_q + row < NOPE, root, clip)
            for q in range(4):
                begin = q * rows + row * heads
                columns = slice(q * quarter, (q + 1) * quarter)
                fresh = turned[begin : begin + heads, :]
                update_ref[layer, row, :, columns] = fresh
                new_weight_ref[layer, row, :, columns] = (
                    weight_ref[layer, row, :, columns] * (1.0 - LEARN_RATE * WEIGHT_DECAY)
                    - step_scale * fresh
                ) * scale

    for kind in "abx":
        for way in range(2):
            for lane in range(2):
                for step in range(hops(way, lane)):
                    ring_copy(kind, way, lane, step).wait_send()
    for place in range(ring):
        for lane in range(2):
            cross_copy(place, lane).wait_send()
    for kind in "ab":
        pair_copy(kind).wait_send()
    @pl.when(works)
    def _():
        @pl.loop(1, group)
        def _(step):
            back_copy(mine, step).wait_send()


def finish(*refs):
    kept, outs, sem = refs[:4], refs[4:8], refs[8]
    copies = [
        pltpu.make_async_copy(src.at[part], dst.at[part], sem.at[number, part])
        for number, (src, dst) in enumerate(zip(kept, outs))
        for part in range(src.shape[0])
    ]
    for copy in copies:
        copy.start()
    for copy in copies:
        copy.wait()


def on_device(latent, query_grad, momentum, weight, max_logit, owner_list):
    group = lax.axis_size("dp")
    layers, heads, rows_q, width = momentum.shape
    mats = layers * heads
    full_rows = rows_q * group
    rows = heads * rows_q
    quarter = width // 4
    half = width // 2
    ring = group // X_HI
    extra = width // 3
    narrow = width - 2 * extra
    wide = half + extra

    by_row = jnp.asarray(reorder_matrix((heads, group, rows_q), (1, 2, 0)), BF16)
    gather = jnp.asarray(reorder_matrix((group, 4, rows_q), (1, 0, 2)), BF16)
    spread = jnp.asarray(reorder_matrix((4, group, rows_q), (1, 0, 2)), BF16)
    split = jnp.asarray(reorder_matrix((4 * rows_q, heads), (1, 0)), BF16)
    join = jnp.asarray(reorder_matrix((heads, 4 * rows_q), (1, 0)), BF16)

    vmem = pl.BlockSpec(memory_space=pltpu.VMEM)
    smem = pl.BlockSpec(memory_space=pltpu.SMEM)
    hbm = pl.BlockSpec(memory_space=pl.ANY)
    by_rows = (layers, rows_q, heads, width)
    dma = pltpu.SemaphoreType.DMA
    new_momentum, owned, update, new_weight = pl.pallas_call(
        functools.partial(kernel, group),
        out_shape=(
            pltpu.VMEM(by_rows, F32),
            pltpu.VMEM((CAP, full_rows, width), BF16),
            pltpu.VMEM(by_rows, F32),
            pltpu.VMEM(by_rows, F32),
        ),
        in_specs=[hbm] * 9 + [vmem, smem],
        out_specs=(vmem, vmem, vmem, vmem),
        scratch_shapes=[
            pltpu.VMEM(by_rows, F32),
            pltpu.VMEM(latent.shape, BF16),
            pltpu.VMEM(query_grad.shape, BF16),
            pltpu.VMEM(by_rows, F32),
            pltpu.VMEM(by_row.shape, BF16),
            pltpu.VMEM(gather.shape, BF16),
            pltpu.VMEM(spread.shape, BF16),
            pltpu.VMEM(split.shape, BF16),
            pltpu.VMEM(join.shape, BF16),
            pltpu.VMEM((heads * full_rows, latent.shape[1]), BF16),
            pltpu.VMEM((group, rows, width), BF16),
            pltpu.VMEM((group, rows, narrow), BF16),
            pltpu.VMEM((2, group, rows, wide), BF16),
            pltpu.VMEM((ring // 2, 2, 2, rows, width), BF16),
            pltpu.VMEM((ring // 2, 2, 2, rows, narrow), BF16),
            pltpu.VMEM((ring // 2, 2, 2, rows, wide), BF16),
            pltpu.VMEM((2, ring, rows, wide), BF16),
            pltpu.VMEM((rows, width), BF16),
            pltpu.VMEM((rows, narrow), BF16),
            pltpu.VMEM((rows, width), F32),
            pltpu.VMEM((4 * rows, quarter), F32),
            pltpu.SMEM((CAP, group), jnp.int32),
            pltpu.VMEM((mats + 1, rows, quarter), BF16),
            pltpu.VMEM((CAP, group, rows, quarter), BF16),
            pltpu.VMEM((CAP, group, rows, quarter), BF16),
            pltpu.VMEM((group * rows, quarter), BF16),
            pltpu.VMEM((group, rows, quarter), BF16),
            pltpu.VMEM((group, rows, quarter), BF16),
            pltpu.VMEM((mats, rows, quarter), BF16),
            dma((13,)),
            dma((ring // 2, 2, 2)),
            dma((ring // 2, 2, 2)),
            dma((ring // 2, 2, 2)),
            dma((ring // 2, 2, 2)),
            dma((ring // 2, 2, 2)),
            dma((ring // 2, 2, 2)),
            dma((ring, 2)),
            dma((ring, 2)),
            dma((2,)),
            dma((2,)),
            dma((CAP, group)),
            dma((CAP, group)),
            dma((mats,)),
            dma((group,)),
            dma((group,)),
            dma((mats,)),
        ],
        compiler_params=pltpu.CompilerParams(
            collective_id=0, has_side_effects=True, vmem_limit_bytes=56 * 2**20
        ),
    )(
        latent,
        query_grad,
        momentum.transpose(0, 2, 1, 3),
        weight.transpose(0, 2, 1, 3),
        by_row,
        gather,
        spread,
        split,
        join,
        max_logit,
        owner_list,
    )

    update, new_weight, new_momentum, owned = pl.pallas_call(
        finish,
        out_shape=(
            jax.ShapeDtypeStruct(by_rows, F32),
            jax.ShapeDtypeStruct(by_rows, F32),
            jax.ShapeDtypeStruct(by_rows, F32),
            jax.ShapeDtypeStruct((CAP, full_rows, width), BF16),
        ),
        in_specs=[hbm] * 4,
        out_specs=(hbm, hbm, hbm, hbm),
        scratch_shapes=[dma((4, layers))],
        compiler_params=pltpu.CompilerParams(vmem_limit_bytes=2 * 2**20),
    )(update, new_weight, new_momentum, owned)
    return (
        update.transpose(0, 2, 1, 3),
        new_weight.transpose(0, 2, 1, 3),
        new_momentum.transpose(0, 2, 1, 3),
        owned[None],
    )


def solution(mesh):
    placed = (
        P(None, "dp", None),
        P(None, "dp", "expert"),
        P(None, "expert", "dp", None),
        P(None, "expert", "dp", None),
        P(None, "expert"),
        P(None, "expert"),
    )
    return jax.shard_map(
        on_device,
        mesh=mesh,
        in_specs=placed,
        out_specs=(
            P(None, "expert", "dp", None),
            P(None, "expert", "dp", None),
            P(None, "expert", "dp", None),
            P("expert", "dp", None, None),
        ),
        check_vma=False,
    )
```

```python
import functools
import math

import jax
import jax.numpy as jnp
import numpy as np
from jax import lax
from jax.experimental import pallas as pl
from jax.experimental.pallas import tpu as pltpu
from jax.sharding import PartitionSpec as P

NOPE = 128
CAP = 2
ITERS = 5
X_HI = 2

DECAY_RATE = 0.95
EPSILON = 1e-07
COEF_LINEAR = 3.4445
COEF_CUBIC = -4.775
COEF_QUINTIC = 2.0315
LEARN_RATE = 0.02
WEIGHT_DECAY = 0.1
CLIP_LIMIT = 100.0
RMS_FACTOR = 0.2

MESH = pl.DeviceIdType.MESH
F32 = jnp.float32
BF16 = jnp.bfloat16


def reorder_matrix(shape, axes):
    picked = np.arange(math.prod(shape)).reshape(shape).transpose(axes).reshape(-1)
    table = np.zeros((picked.size, picked.size), np.float32)
    table[np.arange(picked.size), picked] = 1.0
    return table


def remote(src, dst, send_sem, recv_sem, dp):
    return pltpu.make_async_remote_copy(
        src_ref=src,
        dst_ref=dst,
        send_sem=send_sem,
        recv_sem=recv_sem,
        device_id={"dp": dp},
        device_id_type=MESH,
    )


def parts_of(value, count):
    parts = []
    for _ in range(count):
        parts.append(value.astype(BF16))
        value = value - parts[-1].astype(F32)
    return parts


def part_dot(left, right):
    size = left[0].shape[0]
    count = len(right)
    result = None
    for place in range(count - 1, -1, -1):
        stacked = left[0] if place == count - 1 else jnp.concatenate(left[: count - place], axis=0)
        product = jnp.dot(stacked, right[place], preferred_element_type=F32)
        for row in range(count - place - 1, -1, -1):
            term = product[row * size : (row + 1) * size]
            result = term if result is None else result + term
    return result


def polynomial(gram):
    size = gram.shape[0]
    rows = lax.broadcasted_iota(jnp.int32, (size, size), 0)
    columns = lax.broadcasted_iota(jnp.int32, (size, size), 1)
    eye = jnp.where(rows == columns, 1.0, 0.0).astype(F32)
    total = None
    for sweep in range(ITERS):
        count = 3 if sweep < 3 else 2
        gram_parts = parts_of(gram, count)
        mixing = (
            COEF_LINEAR * eye + COEF_CUBIC * gram + COEF_QUINTIC * part_dot(gram_parts, gram_parts)
        )
        mixing_parts = parts_of(mixing, count)
        if sweep < ITERS - 1:
            gram = part_dot(parts_of(part_dot(mixing_parts, gram_parts), count), mixing_parts)
        total = mixing if total is None else part_dot(parts_of(total, 2), mixing_parts[:2])
    return total


def worker_of(layer, head):
    return 4 * head + (layer if layer < 2 else 2 + head % 2)


def orthogonalize(received, gather_ref, shuffled):
    shuffled[...] = jnp.dot(gather_ref[...], received, preferred_element_type=F32).astype(BF16)
    size = shuffled.shape[0] // 4
    gram = jnp.zeros((size, size), F32)
    for q in range(4):
        piece = shuffled[q * size : (q + 1) * size]
        gram = gram + lax.dot_general(
            piece, piece, (((1,), (1,)), ((), ())), preferred_element_type=F32
        )
    on_diagonal = lax.broadcasted_iota(jnp.int32, gram.shape, 0) == lax.broadcasted_iota(
        jnp.int32, gram.shape, 1
    )
    squares = jnp.sum(
        jnp.sum(jnp.where(on_diagonal, gram, 0.0), axis=1, keepdims=True), axis=0, keepdims=True
    )
    scale = 1.0 / (jnp.sqrt(squares) + EPSILON)
    mixed = polynomial(gram * scale * scale) * scale
    high = mixed.astype(BF16)
    low = (mixed - high.astype(F32)).astype(BF16)
    for q in range(4):
        span = slice(q * size, (q + 1) * size)
        piece = shuffled[span]
        shuffled[span] = (
            jnp.dot(high, piece, preferred_element_type=F32)
            + jnp.dot(low, piece, preferred_element_type=F32)
        ).astype(BF16)


def kernel(
    group,
    latent_hbm, grad_hbm, momentum_hbm, weight_hbm, by_row_hbm, gather_hbm, spread_hbm, split_hbm, join_hbm,
    logit_ref, owner_ref,
    new_momentum_ref, owned_ref, update_ref, new_weight_ref,
    weight_ref,
    latent_ref, grad_ref, momentum_ref, by_row_ref, gather_ref, spread_ref, split_ref, join_ref,
    cot, part_a, part_b, part_x, ring_a, ring_b, ring_x, cross_x, pair_a, pair_b,
    total, turned, pick, blocks, outgoing, incoming, shuffled, worked, back, returned,
    load_sem, send_a, got_a, send_b, got_b, send_x, got_x, send_c, got_c, send_p, got_p,
    send_out, got_out, send_work, got_work, send_back, got_back,
):
    layers, rows_q, heads, width = momentum_ref.shape
    rows = heads * rows_q
    mats = layers * heads
    ring = group // X_HI
    quarter = width // 4
    half = width // 2
    narrow = part_b.shape[-1]
    extra = part_x.shape[-1] - half
    full_rows = rows_q * group
    me = lax.axis_index("dp")
    z = me // X_HI
    side = me % X_HI
    up = lax.rem(z + 1, ring) * X_HI + side
    down = lax.rem(z + ring - 1, ring) * X_HI + side
    partner = z * X_HI + 1 - side

    barrier = pltpu.get_barrier_semaphore()
    for peer in (up, down, partner):
        pl.semaphore_signal(barrier, inc=1, device_id={"dp": peer}, device_id_type=MESH)

    loads = {}
    for number, (name, src, dst) in enumerate(
        [
            ("by_row", by_row_hbm, by_row_ref),
            ("grad0", grad_hbm.at[0], grad_ref.at[0]),
            ("latent0", latent_hbm.at[0], latent_ref.at[0]),
            ("grad2", grad_hbm.at[2], grad_ref.at[2]),
            ("latent2", latent_hbm.at[2], latent_ref.at[2]),
            ("grad1", grad_hbm.at[1], grad_ref.at[1]),
            ("latent1", latent_hbm.at[1], latent_ref.at[1]),
            ("momentum", momentum_hbm, momentum_ref),
            ("split", split_hbm, split_ref),
            ("gather", gather_hbm, gather_ref),
            ("spread", spread_hbm, spread_ref),
            ("join", join_hbm, join_ref),
            ("weight", weight_hbm, weight_ref),
        ]
    ):
        loads[name] = pltpu.make_async_copy(src, dst, load_sem.at[number])
        loads[name].start()

    def products(layer, keep):
        loads["grad%d" % layer].wait()
        cot[...] = lax.dot_general(
            by_row_ref[...], grad_ref[layer], (((1,), (1,)), ((), ())), preferred_element_type=F32
        ).astype(BF16)
        loads["latent%d" % layer].wait()
        for first in range(0, group, 4):
            product = jnp.dot(
                cot[first * rows : (first + 4) * rows], latent_ref[layer], preferred_element_type=F32
            )
            keep(slice(first, first + 4), product.astype(BF16).reshape(4, rows, width))

    def keep_0(blocks_of, product):
        part_a[blocks_of] = product

    def keep_1(blocks_of, product):
        part_b[blocks_of] = product[:, :, :narrow]
        for way in range(2):
            begin = narrow + way * extra
            part_x[way, blocks_of, :, half:] = product[:, :, begin : begin + extra]

    def keep_2(blocks_of, product):
        for way in range(2):
            part_x[way, blocks_of, :, :half] = product[:, :, way * half : (way + 1) * half]

    near, far = ring // 2 - 1, ring // 2

    def hops(way, lane):
        return far if way == lane else near

    def chunk_at(way, distance):
        if way == 0:
            return lax.rem(z + distance, ring)
        return lax.rem(z + ring - distance, ring)

    def ring_copy(kind, way, lane, step):
        chunk = chunk_at(way, hops(way, lane) - step)
        src, dst, send, got = {
            "a": (part_a.at[chunk * X_HI + lane], ring_a, send_a, got_a),
            "b": (part_b.at[chunk * X_HI + lane], ring_b, send_b, got_b),
            "x": (part_x.at[lane, chunk * X_HI + side], ring_x, send_x, got_x),
        }[kind]
        return remote(
            src,
            dst.at[step, way, lane],
            send.at[step, way, lane],
            got.at[step, way, lane],
            up if way == 0 else down,
        )

    cross_order = [(0, far)]
    for distance in range(near, 0, -1):
        cross_order += [(0, distance), (1, distance)]
    cross_order.append((0, 0))

    def cross_copy(place, lane):
        chunk = chunk_at(*cross_order[place])
        return remote(
            part_x.at[lane, chunk * X_HI + 1 - side],
            cross_x.at[lane, chunk],
            send_c.at[place, lane],
            got_c.at[place, lane],
            partner,
        )

    def pair_copy(kind):
        number, src, dst = {"a": (0, part_a, pair_a), "b": (1, part_b, pair_b)}[kind]
        return remote(src.at[partner], dst, send_p.at[number], got_p.at[number], partner)

    def cross(first, last):
        for place in range(first, last):
            for lane in range(2):
                cross_copy(place, lane).start()

    def ring_step(kind, way, lane, step):
        count = hops(way, lane)
        if step >= 0:
            ring_copy(kind, way, lane, step).wait_recv()
        if step == count - 1:
            return
        distance = count - step - 1
        chunk = chunk_at(way, distance)
        if kind == "x":
            place = cross_order.index((0 if distance == far else way, distance))
            cross_copy(place, lane).wait_recv()
            spot = chunk * X_HI + side
            value = part_x[lane, spot].astype(F32) + cross_x[lane, chunk].astype(F32)
            if step >= 0:
                value = value + ring_x[step, way, lane].astype(F32)
            part_x[lane, spot] = value.astype(BF16)
        elif step >= 0:
            mine, came = {"a": (part_a, ring_a), "b": (part_b, ring_b)}[kind]
            spot = chunk * X_HI + lane
            mine[spot] = (mine[spot].astype(F32) + came[step, way, lane].astype(F32)).astype(BF16)
        ring_copy(kind, way, lane, step + 1).start()

    def ring_far(kind, step):
        for way in range(2):
            ring_step(kind, way, way, step)

    def ring_near(kind, step):
        for way in range(2):
            ring_step(kind, way, 1 - way, step)

    def arrived(kind, lane):
        came = {"a": ring_a, "b": ring_b}[kind]
        if isinstance(lane, int):
            up_last, down_last = hops(0, lane) - 1, hops(1, lane) - 1
        else:
            up_last, down_last = far - 1 - lane, near - 1 + lane
        return came[up_last, 0, lane].astype(F32) + came[down_last, 1, lane].astype(F32)

    def pair_step(kind):
        mine = {"a": part_a, "b": part_b}[kind]
        mine[partner] = (mine[partner].astype(F32) + arrived(kind, 1 - side)).astype(BF16)
        pair_copy(kind).start()

    loads["by_row"].wait()
    products(0, keep_0)
    pl.semaphore_wait(barrier, 3)
    ring_far("a", -1)
    ring_near("a", -1)
    products(2, keep_2)
    products(1, keep_1)
    cross(0, 1)
    ring_far("b", -1)
    ring_near("b", -1)
    cross(1, 3)

    owner_of = [owner_ref[m // heads, m % heads] for m in range(mats)]
    slot_of = []
    for m in range(mats):
        slot = jnp.int32(0)
        for earlier in range(m):
            slot = slot + jnp.where(owner_of[earlier] == owner_of[m], 1, 0)
        slot_of.append(slot)

    @pl.loop(0, group)
    def _(owner):
        for slot in range(CAP):
            found = jnp.int32(mats)
            for m in range(mats):
                found = jnp.where((owner_of[m] == owner) & (slot_of[m] == slot), m, found)
            pick[slot, owner] = found

    ring_far("a", 0)
    ring_near("a", 0)
    ring_far("b", 0)
    ring_near("b", 0)
    ring_far("x", -1)
    cross(3, 5)
    ring_far("a", 1)
    ring_near("a", 1)
    ring_far("b", 1)
    ring_near("b", 1)
    ring_far("x", 0)
    ring_near("x", -1)
    cross(5, 7)
    ring_far("a", 2)
    ring_near("a", 2)
    ring_far("b", 2)
    ring_near("b", 2)
    ring_far("x", 1)
    ring_near("x", 0)
    cross(7, 8)
    ring_far("a", 3)
    pair_step("a")
    ring_far("b", 3)
    pair_step("b")
    ring_far("x", 2)
    ring_near("x", 1)
    ring_far("x", 3)
    ring_near("x", 2)
    for lane in range(2):
        cross_copy(ring - 1, lane).wait_recv()

    loads["momentum"].wait()
    loads["split"].wait()

    def last_sum(kind):
        mine, other = {"a": (part_a, pair_a), "b": (part_b, pair_b)}[kind]
        pair_copy(kind).wait_recv()
        return mine[me].astype(F32) + arrived(kind, side) + other[...].astype(F32)

    def last_sum_x(lane, columns):
        return (
            part_x[lane, me, :, columns].astype(F32)
            + cross_x[lane, z, :, columns].astype(F32)
            + ring_x[hops(0, lane) - 1, 0, lane, :, columns].astype(F32)
            + ring_x[hops(1, lane) - 1, 1, lane, :, columns].astype(F32)
        )

    def work_of(device):
        return jnp.minimum(device % 4, 2) * heads + device // 4

    def work_copy(layer, head):
        mat = layer * heads + head
        return remote(
            blocks.at[mat], worked.at[me], send_work.at[mat], got_work.at[me], worker_of(layer, head)
        )

    def work_from(source):
        return remote(worked.at[source], worked.at[source], send_work.at[0], got_work.at[source], up)

    lot = me % 4
    works = (lot < 2) | (lot == 2 + (me // 4) % 2)
    mine = work_of(me)

    for layer in (2, 0, 1):
        if layer == 2:
            for way in range(2):
                total[:, way * half : (way + 1) * half] = last_sum_x(way, slice(0, half))
        elif layer == 0:
            total[...] = last_sum("a")
        else:
            total[:, :narrow] = last_sum("b")
            for way in range(2):
                begin = narrow + way * extra
                total[:, begin : begin + extra] = last_sum_x(way, slice(half, half + extra))
        for row in range(rows_q):
            span = slice(row * heads, (row + 1) * heads)
            fresh = DECAY_RATE * momentum_ref[layer, row] + total[span, :]
            new_momentum_ref[layer, row] = fresh
            total[span, :] = fresh
        stacked = jnp.concatenate(
            [total[:, q * quarter : (q + 1) * quarter].astype(BF16) for q in range(4)], axis=0
        )
        blocks[layer * heads : (layer + 1) * heads] = (
            jnp.dot(split_ref[...], stacked, preferred_element_type=F32)
            .astype(BF16)
            .reshape(heads, rows, quarter)
        )
        for head in range(heads):

            @pl.when(me != worker_of(layer, head))
            def _():
                work_copy(layer, head).start()

    blocks[mats] = jnp.zeros((rows, quarter), BF16)


    def back_copy(mat, step):
        peer = lax.rem(me + step, group)
        return remote(back.at[peer], returned.at[mat], send_back.at[step], got_back.at[mat], peer)

    def out_copy(slot, step):
        peer = lax.rem(me + step, group)
        return remote(
            outgoing.at[slot, peer],
            incoming.at[slot, me],
            send_out.at[slot, step],
            got_out.at[slot, step],
            peer,
        )

    def send_slot(slot):
        @pl.loop(1, group)
        def _(step):
            peer = lax.rem(me + step, group)
            outgoing[slot, peer] = blocks[pick[slot, peer]]
            out_copy(slot, step).start()

        incoming[slot, me] = blocks[pick[slot, me]]

    def work_left():
        for layer in range(layers):
            for head in range(heads):

                @pl.when(me != worker_of(layer, head))
                def _():
                    work_copy(layer, head).wait_send()

    def slot_left(slot, first, last):
        @pl.loop(first, last)
        def _(step):
            out_copy(slot, step).wait_send()

    def do_work():
        @pl.when(works)
        def _():
            worked[me] = blocks[mine]

            @pl.loop(1, group)
            def _(step):
                work_from(lax.rem(me + step, group)).wait_recv()

            orthogonalize(worked[...].reshape(group * rows, quarter), gather_ref, shuffled)
            back[...] = (
                jnp.dot(spread_ref[...], shuffled[...], preferred_element_type=F32)
                .astype(BF16)
                .reshape(group, rows, quarter)
            )

    def post_back():
        @pl.when(works)
        def _():
            @pl.loop(1, group)
            def _(step):
                back_copy(mine, step).start()

            returned[mine] = back[me]

    loads["gather"].wait()
    loads["spread"].wait()
    loads["join"].wait()

    def own_slot(slot):
        @pl.loop(1, group)
        def _(step):
            out_copy(slot, step).wait_recv()

        orthogonalize(incoming[slot].reshape(group * rows, quarter), gather_ref, shuffled)
        for q in range(4):
            owned_ref[slot, :, q * quarter : (q + 1) * quarter] = shuffled[
                q * full_rows : (q + 1) * full_rows
            ]

    send_slot(0)
    work_left()
    send_slot(1)
    do_work()
    own_slot(0)
    slot_left(0, 1, group)
    slot_left(1, 1, group)
    post_back()
    own_slot(1)

    loads["weight"].wait()
    step_scale = LEARN_RATE * RMS_FACTOR * math.sqrt(max(full_rows, width))
    heads_diagonal = lax.broadcasted_iota(jnp.int32, (heads, heads), 0) == lax.broadcasted_iota(
        jnp.int32, (heads, heads), 1
    )
    for layer in range(layers):
        for head in range(heads):
            mat = layer * heads + head

            @pl.when(me != worker_of(layer, head))
            def _():
                back_copy(mat, 1).wait_recv()

        gathered = returned[layer * heads : (layer + 1) * heads].reshape(4 * rows, quarter)
        turned[...] = jnp.dot(join_ref[...], gathered, preferred_element_type=F32)
        clip = jnp.minimum(1.0, CLIP_LIMIT / logit_ref[layer : layer + 1, :])
        clip = jnp.sum(
            jnp.where(heads_diagonal, jnp.broadcast_to(clip, (heads, heads)), 0.0),
            axis=1,
            keepdims=True,
        )
        root = jnp.sqrt(clip)
        for row in range(rows_q):
            scale = jnp.where(me * rows_q + row < NOPE, root, clip)
            for q in range(4):
                begin = q * rows + row * heads
                columns = slice(q * quarter, (q + 1) * quarter)
                fresh = turned[begin : begin + heads, :]
                update_ref[layer, row, :, columns] = fresh
                new_weight_ref[layer, row, :, columns] = (
                    weight_ref[layer, row, :, columns] * (1.0 - LEARN_RATE * WEIGHT_DECAY)
                    - step_scale * fresh
                ) * scale

    for kind in "abx":
        for way in range(2):
            for lane in range(2):
                for step in range(hops(way, lane)):
                    ring_copy(kind, way, lane, step).wait_send()
    for place in range(ring):
        for lane in range(2):
            cross_copy(place, lane).wait_send()
    for kind in "ab":
        pair_copy(kind).wait_send()
    @pl.when(works)
    def _():
        @pl.loop(1, group)
        def _(step):
            back_copy(mine, step).wait_send()


def finish(*refs):
    kept, outs, sem = refs[:4], refs[4:8], refs[8]
    copies = [
        pltpu.make_async_copy(src.at[part], dst.at[part], sem.at[number, part])
        for number, (src, dst) in enumerate(zip(kept, outs))
        for part in range(src.shape[0])
    ]
    for copy in copies:
        copy.start()
    for copy in copies:
        copy.wait()


def on_device(latent, query_grad, momentum, weight, max_logit, owner_list):
    group = lax.axis_size("dp")
    layers, heads, rows_q, width = momentum.shape
    mats = layers * heads
    full_rows = rows_q * group
    rows = heads * rows_q
    quarter = width // 4
    half = width // 2
    ring = group // X_HI
    extra = width // 4
    narrow = width - 2 * extra
    wide = half + extra

    by_row = jnp.asarray(reorder_matrix((heads, group, rows_q), (1, 2, 0)), BF16)
    gather = jnp.asarray(reorder_matrix((group, 4, rows_q), (1, 0, 2)), BF16)
    spread = jnp.asarray(reorder_matrix((4, group, rows_q), (1, 0, 2)), BF16)
    split = jnp.asarray(reorder_matrix((4 * rows_q, heads), (1, 0)), BF16)
    join = jnp.asarray(reorder_matrix((heads, 4 * rows_q), (1, 0)), BF16)

    vmem = pl.BlockSpec(memory_space=pltpu.VMEM)
    smem = pl.BlockSpec(memory_space=pltpu.SMEM)
    hbm = pl.BlockSpec(memory_space=pl.ANY)
    by_rows = (layers, rows_q, heads, width)
    dma = pltpu.SemaphoreType.DMA
    new_momentum, owned, update, new_weight = pl.pallas_call(
        functools.partial(kernel, group),
        out_shape=(
            pltpu.VMEM(by_rows, F32),
            pltpu.VMEM((CAP, full_rows, width), BF16),
            pltpu.VMEM(by_rows, F32),
            pltpu.VMEM(by_rows, F32),
        ),
        in_specs=[hbm] * 9 + [vmem, smem],
        out_specs=(vmem, vmem, vmem, vmem),
        scratch_shapes=[
            pltpu.VMEM(by_rows, F32),
            pltpu.VMEM(latent.shape, BF16),
            pltpu.VMEM(query_grad.shape, BF16),
            pltpu.VMEM(by_rows, F32),
            pltpu.VMEM(by_row.shape, BF16),
            pltpu.VMEM(gather.shape, BF16),
            pltpu.VMEM(spread.shape, BF16),
            pltpu.VMEM(split.shape, BF16),
            pltpu.VMEM(join.shape, BF16),
            pltpu.VMEM((heads * full_rows, latent.shape[1]), BF16),
            pltpu.VMEM((group, rows, width), BF16),
            pltpu.VMEM((group, rows, narrow), BF16),
            pltpu.VMEM((2, group, rows, wide), BF16),
            pltpu.VMEM((ring // 2, 2, 2, rows, width), BF16),
            pltpu.VMEM((ring // 2, 2, 2, rows, narrow), BF16),
            pltpu.VMEM((ring // 2, 2, 2, rows, wide), BF16),
            pltpu.VMEM((2, ring, rows, wide), BF16),
            pltpu.VMEM((rows, width), BF16),
            pltpu.VMEM((rows, narrow), BF16),
            pltpu.VMEM((rows, width), F32),
            pltpu.VMEM((4 * rows, quarter), F32),
            pltpu.SMEM((CAP, group), jnp.int32),
            pltpu.VMEM((mats + 1, rows, quarter), BF16),
            pltpu.VMEM((CAP, group, rows, quarter), BF16),
            pltpu.VMEM((CAP, group, rows, quarter), BF16),
            pltpu.VMEM((group * rows, quarter), BF16),
            pltpu.VMEM((group, rows, quarter), BF16),
            pltpu.VMEM((group, rows, quarter), BF16),
            pltpu.VMEM((mats, rows, quarter), BF16),
            dma((13,)),
            dma((ring // 2, 2, 2)),
            dma((ring // 2, 2, 2)),
            dma((ring // 2, 2, 2)),
            dma((ring // 2, 2, 2)),
            dma((ring // 2, 2, 2)),
            dma((ring // 2, 2, 2)),
            dma((ring, 2)),
            dma((ring, 2)),
            dma((2,)),
            dma((2,)),
            dma((CAP, group)),
            dma((CAP, group)),
            dma((mats,)),
            dma((group,)),
            dma((group,)),
            dma((mats,)),
        ],
        compiler_params=pltpu.CompilerParams(
            collective_id=0, has_side_effects=True, vmem_limit_bytes=56 * 2**20
        ),
    )(
        latent,
        query_grad,
        momentum.transpose(0, 2, 1, 3),
        weight.transpose(0, 2, 1, 3),
        by_row,
        gather,
        spread,
        split,
        join,
        max_logit,
        owner_list,
    )

    update, new_weight, new_momentum, owned = pl.pallas_call(
        finish,
        out_shape=(
            jax.ShapeDtypeStruct(by_rows, F32),
            jax.ShapeDtypeStruct(by_rows, F32),
            jax.ShapeDtypeStruct(by_rows, F32),
            jax.ShapeDtypeStruct((CAP, full_rows, width), BF16),
        ),
        in_specs=[hbm] * 4,
        out_specs=(hbm, hbm, hbm, hbm),
        scratch_shapes=[dma((4, layers))],
        compiler_params=pltpu.CompilerParams(vmem_limit_bytes=2 * 2**20),
    )(update, new_weight, new_momentum, owned)
    return (
        update.transpose(0, 2, 1, 3),
        new_weight.transpose(0, 2, 1, 3),
        new_momentum.transpose(0, 2, 1, 3),
        owned[None],
    )


def solution(mesh):
    placed = (
        P(None, "dp", None),
        P(None, "dp", "expert"),
        P(None, "expert", "dp", None),
        P(None, "expert", "dp", None),
        P(None, "expert"),
        P(None, "expert"),
    )
    return jax.shard_map(
        on_device,
        mesh=mesh,
        in_specs=placed,
        out_specs=(
            P(None, "expert", "dp", None),
            P(None, "expert", "dp", None),
            P(None, "expert", "dp", None),
            P("expert", "dp", None, None),
        ),
        check_vma=False,
    )
```
